128 devices in a mesh: ctx: 32 (over x, y, core), kvh: 4 (over z).
Axes of the slice: x: 4, y: 4, z: 4, core: 2. Of those that a mesh axis runs over, the one named last changes fastest.
Arguments:
- queries: bfloat16 [49152, 2048], P('ctx', 'kvh'), may hold values from -44 to 44
- key_rows: bfloat16 [49152, 512], P('ctx', 'kvh'), may hold values from -10 to 10
- value_rows: bfloat16 [49152, 512], P('ctx', 'kvh'), may hold values from -6 to 6
- out_grad: bfloat16 [49152, 2048], P('ctx', 'kvh'), may hold values from -6 to 6
- picked: int32 [96, 2], replicated, may hold values from 0 to 95, as said below
Outputs:
- query_grad: bfloat16 [49152, 2048], P(('ctx', 'kvh'))
- key_grad: bfloat16 [49152, 512], P(('ctx', 'kvh'))
- value_grad: bfloat16 [49152, 512], P(('ctx', 'kvh'))
The draws below stay inside these ranges and needn't reach their ends.
Inputs may be any that keep to these rules, and one draw needn't show every extreme that they name: `picked`: row q names key blocks before q, or q itself for no pick; the two differ unless both are q. All picks of the 3 query blocks of one index of ctx that lie in blocks of another index name one and the same block of that index. The last block's second pick is dead.
All inputs are finite; a program needn't handle non-finite values.
Results may differ from the reference program's by a relative error of at most 0.0096.
Values may be sent and summed in bfloat16 or wider, within the bound.
A program may use at most 192 MiB of HBM per device.

```python
import jax
import jax.numpy as jnp
from jax import lax

QHEADS = 16
KVHEADS = 4
HEAD = 128
BLK = 512
TOPK = 3
BLK_DEV = 3
NBLK = 96
TOKENS = 49152
N_CTX = 32


def shared_rows(key):
    base_rows = jnp.clip(jax.random.normal(key, (TOKENS, KVHEADS * HEAD), jnp.float32), -4.0, 4.0)
    return base_rows


def draw_key_rows(key, part):
    base_rows = shared_rows(key)
    result = base_rows
    return result.astype(jnp.bfloat16)


def draw_queries(key, part):
    key = jax.random.fold_in(key, 11)
    own_rows = jnp.clip(jax.random.normal(key, (TOKENS, QHEADS * HEAD), jnp.float32), -4.0, 4.0)
    return own_rows.astype(jnp.bfloat16)


def draw_picked(key, part):
    key = jax.random.fold_in(key, 5)
    key_one, key_two = jax.random.split(key, 2)
    row_ids = jnp.arange(NBLK)
    device_of = row_ids // BLK_DEV
    position = row_ids % BLK_DEV
    partners = jnp.arange(N_CTX)
    offsets = jax.random.randint(key_one, (N_CTX, N_CTX), 0, BLK_DEV)
    chosen_block = jnp.where(partners[None, :] == 0, 0, partners[None, :] * BLK_DEV + offsets)
    earlier = partners[None, :] < partners[:, None]
    wrap_pick = (partners[:, None] == N_CTX - 1) & (partners[None, :] == 0)
    ranking = jax.random.randint(key_two, (N_CTX, N_CTX), 0, 1 << 20) * N_CTX + partners[None, :] + earlier.astype(jnp.int32) * (1 << 26) + wrap_pick.astype(jnp.int32) * (1 << 27)
    order = jnp.argsort(-ranking, axis=1, stable=True).astype(jnp.int32)
    safe_count = jnp.maximum(device_of, 1)
    slot_one = 2 * position % safe_count
    slot_two = (2 * position + 1) % safe_count
    partner_one = order[device_of, slot_one]
    partner_two = order[device_of, slot_two]
    far_one = chosen_block[device_of, partner_one]
    far_two = chosen_block[device_of, partner_two]
    near_one = jnp.where(position >= 1, row_ids - 1, row_ids)
    near_two = jnp.where(position >= 2, row_ids - 2, row_ids)
    first = jnp.where(device_of >= 1, far_one, near_one)
    second = jnp.where(device_of >= 2, far_two, jnp.where(device_of == 1, near_one, near_two))
    second = jnp.where(row_ids == NBLK - 1, row_ids, second)
    return jnp.stack([first, second], axis=1).astype(jnp.int32)


def block_scale(key, extent, shards, least, largest):
    def one(axis_at, shards_of):
        steps = jax.random.uniform(jax.random.fold_in(jax.random.fold_in(key, 6), axis_at), (shards_of,), jnp.float32, least / len(shards), largest / len(shards))
        return jnp.repeat(jnp.exp(steps), extent[axis_at] // shards_of).reshape((-1,) + (1,) * (len(extent) - axis_at - 1))

    level = one(*shards[0])
    for cut in shards[1:]:
        level = level * one(*cut)
    return level


def normal_values(stream_key, extent, spread, reach, cuts=(), held_as=jnp.bfloat16):
    factor_of = block_scale(stream_key, extent, cuts, -0.22, 0.18) if cuts else 1.0
    values = jax.random.normal(stream_key, extent, jnp.float32) * spread * factor_of
    return jnp.minimum(jnp.maximum(values, -reach), reach).astype(held_as)


def setup_inputs(seed: int = 0) -> dict:
    arg_keys = jax.random.split(jax.random.key(seed), 6)
    return {
        "queries": draw_queries(jax.random.fold_in(arg_keys[5], 71), 0),
        "key_rows": draw_key_rows(jax.random.fold_in(arg_keys[5], 71), 0),
        "value_rows": normal_values(arg_keys[2], (TOKENS, KVHEADS * HEAD), 1.0, 6.0, ((0, 32), (1, 4))),
        "out_grad": normal_values(arg_keys[3], (TOKENS, QHEADS * HEAD), 1.0, 6.0, ((0, 32), (1, 4))),
        "picked": draw_picked(jax.random.fold_in(arg_keys[5], 71), 0),
    }


def tile_grads(query_tile, grad_tile, key_tiles, value_tiles, alive_mask):
    block_len = query_tile.shape[0]
    scaling = 1.0 / (HEAD ** 0.5)
    query_wide = query_tile.astype(jnp.float32)
    grad_wide = grad_tile.astype(jnp.float32)
    key_wide = key_tiles.astype(jnp.float32)
    value_wide = value_tiles.astype(jnp.float32)
    scores = jnp.einsum("acgd,jbcd->acgjb", query_wide, key_wide) * scaling
    row_ids = jnp.arange(block_len)
    causal = row_ids[None, :] <= row_ids[:, None]
    first_pick = jnp.arange(key_tiles.shape[0]) == 0
    allowed = jnp.where(first_pick[None, :, None], causal[:, None, :], alive_mask[None, :, None])
    scores = jnp.where(allowed[:, None, None, :, :], scores, -jnp.inf)
    row_top = jnp.max(scores, axis=(3, 4), keepdims=True)
    log_total = row_top + jnp.log(jnp.sum(jnp.exp(scores - row_top), axis=(3, 4), keepdims=True))
    weights = jnp.exp(scores - log_total)
    weights_low = lax.optimization_barrier(weights.astype(jnp.bfloat16)).astype(jnp.float32)
    attn_out = jnp.einsum("acgjb,jbcd->acgd", weights_low, value_wide)
    row_delta = jnp.sum(grad_wide * attn_out, axis=-1)
    weight_grad = jnp.einsum("acgd,jbcd->acgjb", grad_wide, value_wide)
    score_grad = (weights * (weight_grad - row_delta[..., None, None]) * scaling).astype(jnp.bfloat16)
    score_grad = lax.optimization_barrier(score_grad).astype(jnp.float32)
    query_part = jnp.einsum("acgjb,jbcd->acgd", score_grad, key_wide).astype(jnp.bfloat16)
    key_part = jnp.einsum("acgjb,acgd->jbcd", score_grad, query_wide)
    value_part = jnp.einsum("acgjb,acgd->jbcd", weights_low, grad_wide)
    return query_part, key_part, value_part


def reference(queries, key_rows, value_rows, out_grad, picked):
    group_size = QHEADS // KVHEADS

    def per_block(state, block_id):
        key_acc, value_acc = state
        picks_here = picked[block_id]
        key_ids = jnp.concatenate([block_id[None], picks_here]).astype(jnp.int32)
        alive_mask = jnp.concatenate([jnp.array([True]), picks_here != block_id])
        start = (block_id * BLK).astype(jnp.int32)
        query_tile = lax.dynamic_slice_in_dim(queries, start, BLK, 0).reshape(BLK, KVHEADS, group_size, HEAD)
        grad_tile = lax.dynamic_slice_in_dim(out_grad, start, BLK, 0).reshape(BLK, KVHEADS, group_size, HEAD)
        key_tiles = jnp.stack([lax.dynamic_slice_in_dim(key_rows, (key_ids[member] * BLK).astype(jnp.int32), BLK, 0) for member in range(TOPK)])
        value_tiles = jnp.stack([lax.dynamic_slice_in_dim(value_rows, (key_ids[member] * BLK).astype(jnp.int32), BLK, 0) for member in range(TOPK)])
        key_tiles = key_tiles.reshape(TOPK, BLK, KVHEADS, HEAD)
        value_tiles = value_tiles.reshape(TOPK, BLK, KVHEADS, HEAD)
        query_part, key_part, value_part = tile_grads(query_tile, grad_tile, key_tiles, value_tiles, alive_mask)
        for member in range(TOPK):
            offset = (key_ids[member] * BLK).astype(jnp.int32)
            old_keys = lax.dynamic_slice_in_dim(key_acc, offset, BLK, 0)
            key_acc = lax.dynamic_update_slice_in_dim(key_acc, old_keys + key_part[member].reshape(BLK, -1), offset, 0)
            old_values = lax.dynamic_slice_in_dim(value_acc, offset, BLK, 0)
            value_acc = lax.dynamic_update_slice_in_dim(value_acc, old_values + value_part[member].reshape(BLK, -1), offset, 0)
        return (key_acc, value_acc), query_part.reshape(BLK, -1)

    start_state = (jnp.zeros((TOKENS, KVHEADS * HEAD), jnp.float32), jnp.zeros((TOKENS, KVHEADS * HEAD), jnp.float32))
    (key_acc, value_acc), query_parts = lax.scan(per_block, start_state, jnp.arange(NBLK, dtype=jnp.int32))
    return query_parts.reshape(TOKENS, QHEADS * HEAD), key_acc.astype(jnp.bfloat16), value_acc.astype(jnp.bfloat16)
```

```python
import functools

import jax
import jax.numpy as jnp
from jax import lax
from jax.experimental import pallas as pl
from jax.experimental.pallas import tpu as pltpu
from jax.sharding import PartitionSpec as P

HEAD = 128
BLK = 512
SIDE = 4
ROW = 6
LINE = SIDE * ROW
SCALE = 1.0 / HEAD**0.5
LOG2E = 1.4426950408889634
BIG = 3.0e38
MESH = pl.DeviceIdType.MESH
F32 = jnp.float32
LOW = jnp.bfloat16
VMEM_LIMIT = 56 * 2**20


def place():
    index = lax.axis_index("ctx")
    x, y, c = index // 8, (index // 2) % 4, index % 2
    return x, y, c, lax.axis_index("kvh")


def lines(x, y, c):
    return x * (1 - c) + y * c, y * (1 - c) + x * c


def on_first(x, y, c, z, o):
    xx = (x + o * (1 - c)) % SIDE
    yy = (y + o * c) % SIDE
    return (xx * 8 + yy * 2 + c, z)


def on_second(x, y, c, z, o):
    xx = (x + o * c) % SIDE
    yy = (y + o * (1 - c)) % SIDE
    return (xx * 8 + yy * 2 + c, z)


def layout(cap):
    at = {}
    at["send"] = 0
    at["own"] = at["send"] + 3 * cap
    at["own_far"] = at["own"] + 6
    at["sib"] = at["own_far"] + 6
    at["sib_far"] = at["sib"] + 6
    at["pack"] = at["sib_far"] + 6
    at["acc"] = at["pack"] + 2 * 3 * cap
    at["attend"] = at["acc"] + 5 * LINE
    at["size"] = at["attend"] + 12
    return at


def plan_kernel(cap, where, picked, plan, mark, part_of):
    at = layout(cap)
    index = where[0]
    x, y, c = index // 8, (index // 2) % 4, index % 2
    a, b = lines(x, y, c)
    my_chip = x * 4 + y

    def second_of(block):
        return ((block // ROW) % 4) * (1 - c) + (block // LINE) * c

    def slot24(block):
        first = (block // LINE) * (1 - c) + ((block // ROW) % 4) * c
        return first * ROW + block % ROW

    def fill(start, count, value):
        def body(k, _):
            plan[start + k] = value
            return 0

        lax.fori_loop(0, count, body, 0, unroll=6)

    fill(at["send"], 3 * cap, 0)
    fill(at["pack"], 6 * cap, 12)

    def clear(k, _):
        mark[k] = 0
        part_of[2 * k] = 12
        part_of[2 * k + 1] = 12
        return 0

    lax.fori_loop(0, 7 * LINE, clear, 0, unroll=8)

    for o in (1, 2, 3):
        other = (b + o) % 4
        chip = (x * 4 + other) * (1 - c) + (other * 4 + y) * c

        def see(k, _):
            block = picked[chip * 12 + k]

            @pl.when(second_of(block) == b)
            def _():
                mark[(3 + o) * LINE + slot24(block)] = 1

            return 0

        lax.fori_loop(0, 12, see, 0, unroll=4)

        def number(t, count):
            hit = mark[(3 + o) * LINE + t]

            @pl.when(hit == 1)
            def _():
                plan[at["send"] + (o - 1) * cap + count] = t

            plan[at["acc"] + 5 * t + o - 1] = lax.select(
                hit == 1, (o - 1) * cap + count, 3 * cap
            )
            return count + hit

        lax.fori_loop(0, LINE, number, 0, unroll=4)

    def want(k, _):
        core = 1 - k // 6
        pick = 5 - k % 6
        owner = my_chip * 2 + core
        block = picked[owner * 6 + pick]
        o = (second_of(block) - b + 4) % 4
        t = o * LINE + slot24(block)
        mark[t] = 1

        @pl.when(block // 3 != owner)
        def _():
            part_of[2 * t + lax.select(core == c, 0, 1)] = pick + lax.select(core == c, 0, 6)

        return 0

    lax.fori_loop(0, 12, want, 0, unroll=4)

    def home(t, _):
        plan[at["acc"] + 5 * t + 3] = part_of[2 * t]
        plan[at["acc"] + 5 * t + 4] = part_of[2 * t + 1]
        return 0

    lax.fori_loop(0, LINE, home, 0, unroll=4)
    for o in (1, 2, 3):

        def number(t, count):
            hit = mark[o * LINE + t]
            mark[o * LINE + t] = count

            @pl.when(hit == 1)
            def _():
                start = at["pack"] + 2 * ((o - 1) * cap + count)
                plan[start] = part_of[2 * (o * LINE + t)]
                plan[start + 1] = part_of[2 * (o * LINE + t) + 1]

            return count + hit

        lax.fori_loop(0, LINE, number, 0, unroll=4)

    for name, core in (("own", c), ("sib", 1 - c)):

        def find(k, _):
            block = picked[(my_chip * 2 + core) * 6 + k]
            o = (second_of(block) - b + 4) % 4
            t = slot24(block)
            plan[at[name] + k] = t
            plan[at[name + "_far"] + k] = lax.select(
                o == 0, -1, (lax.max(o, 1) - 1) * cap + mark[o * LINE + t]
            )
            return 0

        lax.fori_loop(0, 6, find, 0, unroll=2)

    def target(k, _):
        block = picked[index * 6 + k]
        query = index * 3 + k // 2

        def back(s, best):
            other = 5 - s
            return lax.select(picked[index * 6 + other] == block, other, best)

        first = lax.fori_loop(0, 6, back, k, unroll=6)
        plan[at["attend"] + k] = lax.select(block // 3 == index, block % 3, 3 + first)
        plan[at["attend"] + 6 + k] = lax.select(block == query, 0, 1)
        return 0

    lax.fori_loop(0, 6, target, 0)


def make_plan(cap, picked):
    where = lax.axis_index("ctx").reshape(1).astype(jnp.int32)
    smem = pl.BlockSpec(memory_space=pltpu.SMEM)
    return pl.pallas_call(
        functools.partial(plan_kernel, cap),
        out_shape=jax.ShapeDtypeStruct((layout(cap)["size"],), jnp.int32),
        in_specs=[smem, smem],
        out_specs=smem,
        scratch_shapes=[pltpu.SMEM((7 * LINE,), jnp.int32), pltpu.SMEM((14 * LINE,), jnp.int32)],
        name="plan",
    )(where, picked.reshape(-1))


def remote(src, dst, sends, recvs, k, device):
    return pltpu.make_async_remote_copy(
        src_ref=src,
        dst_ref=dst,
        send_sem=sends.at[k],
        recv_sem=recvs.at[k],
        device_id=device,
        device_id_type=MESH,
    )


def greet(devices):
    barrier = pltpu.get_barrier_semaphore()
    for device in devices:
        pl.semaphore_signal(barrier, inc=1, device_id=device, device_id_type=MESH)
    pl.semaphore_wait(barrier, len(devices))


def fetch_kernel(cap, plan, keys, values, out, pair, near, far, packed, give, take, sends, recvs):
    at = layout(cap)
    x, y, c, z = place()
    a, b = lines(x, y, c)
    sibling = (x * 8 + y * 2 + 1 - c, z)
    up, down = on_first(x, y, c, z, 1), on_first(x, y, c, z, 3)
    greet([sibling, up, down] + [on_second(x, y, c, z, o) for o in (1, 2, 3)])

    for t in range(3):
        pair[0, t] = keys[t * BLK : (t + 1) * BLK]
        pair[1, t] = values[t * BLK : (t + 1) * BLK]
    mine = near.at[pl.ds(a * ROW + c * 3, 3)]
    theirs = near.at[pl.ds(a * ROW + (1 - c) * 3, 3)]
    swap = remote(pair.at[1 - c], near.at[pl.ds(b * ROW + c * 3, 3)], sends, recvs, 0, sibling)
    swap.start()
    for t in range(3):
        near[a * ROW + c * 3 + t] = pair[c, t]
    copies = [
        remote(mine, mine, sends, recvs, 1, up),
        remote(mine, mine, sends, recvs, 2, down),
    ]
    copies[0].start()
    copies[1].start()
    swap.wait_recv()
    copies += [
        remote(theirs, theirs, sends, recvs, 3, up),
        remote(theirs, theirs, sends, recvs, 4, down),
    ]
    copies[3].start()
    copies[2].start()
    copies[0].wait_recv()
    below = near.at[pl.ds(((a + 3) % 4) * ROW + c * 3, 3)]
    copies.append(remote(below, below, sends, recvs, 5, up))
    copies[4].start()
    copies[3].wait_recv()
    above = near.at[pl.ds(((a + 1) % 4) * ROW + (1 - c) * 3, 3)]
    copies.append(remote(above, above, sends, recvs, 6, down))
    copies[5].start()
    for k in (1, 2, 4, 5):
        copies[k].wait_recv()

    passes = []
    for o in (2, 1, 3):

        def pack(s, _):
            packed[(o - 1) * cap + s] = near[plan[at["send"] + (o - 1) * cap + s]]
            return 0

        lax.fori_loop(0, cap, pack, 0)
        copy = remote(
            packed.at[pl.ds((o - 1) * cap, cap)],
            far.at[pl.ds((3 - o) * cap, cap)],
            sends,
            recvs,
            6 + o,
            on_second(x, y, c, z, o),
        )
        copy.start()
        passes.append(copy)
    for copy in passes:
        copy.wait_recv()

    def pick(name, k):
        from_far = plan[at[name + "_far"] + k]
        return jnp.where(
            from_far >= 0, far[lax.max(from_far, 0)], near[plan[at[name] + k]]
        )

    def give_one(k, _):
        give[k] = pick("sib", k)
        return 0

    lax.fori_loop(0, 6, give_one, 0)
    last = remote(give, take, sends, recvs, 10, sibling)
    last.start()

    def own_one(k, _):
        out[c, k] = pick("own", k)
        return 0

    lax.fori_loop(0, 6, own_one, 0)
    last.wait_recv()
    for k in range(6):
        out[1 - c, k] = take[k]
    for copy in [swap] + copies + passes + [last]:
        copy.wait_send()


def fetch(cap, plan, keys, values):
    vmem = pl.BlockSpec(memory_space=pltpu.VMEM)
    tile = (BLK, HEAD)
    return pl.pallas_call(
        functools.partial(fetch_kernel, cap),
        out_shape=jax.ShapeDtypeStruct((2, 6) + tile, LOW),
        in_specs=[pl.BlockSpec(memory_space=pltpu.SMEM), vmem, vmem],
        out_specs=vmem,
        scratch_shapes=[
            pltpu.VMEM((2, 3) + tile, LOW),
            pltpu.VMEM((LINE,) + tile, LOW),
            pltpu.VMEM((3 * cap,) + tile, LOW),
            pltpu.VMEM((3 * cap,) + tile, LOW),
            pltpu.VMEM((6,) + tile, LOW),
            pltpu.VMEM((6,) + tile, LOW),
            pltpu.SemaphoreType.DMA((11,)),
            pltpu.SemaphoreType.DMA((11,)),
        ],
        compiler_params=pltpu.CompilerParams(
            collective_id=0, has_side_effects=True, vmem_limit_bytes=VMEM_LIMIT
        ),
        name="fetch",
    )(plan, keys, values)


def dot(left, right, left_dim, right_dim):
    return lax.dot_general(
        left, right, (((left_dim,), (right_dim,)), ((), ())), preferred_element_type=F32
    )


def head_step(query, grad, keys, values, live, tile):
    weights_low = [[], [], []]
    score_grads = [[], [], []]
    query_grads = []
    for r in range(BLK // tile):
        rows = slice(r * tile, (r + 1) * tile)
        seen = (r + 1) * tile
        ks = [keys[0][:seen], keys[1], keys[2]]
        vs = [values[0][:seen], values[1], values[2]]
        scores = [dot(k, query[rows], 1, 1) for k in ks]
        key_at = lax.broadcasted_iota(jnp.int32, (tile, tile), 0)
        row_at = lax.broadcasted_iota(jnp.int32, (tile, tile), 1)
        corner = jnp.where(key_at <= row_at, scores[0][seen - tile :], -BIG)
        scores[0] = corner if r == 0 else jnp.concatenate([scores[0][: seen - tile], corner], 0)
        weight_grads = [dot(v, grad[rows], 1, 1) for v in vs]
        tops = [jnp.max(s, axis=0, keepdims=True) for s in scores]
        top = tops[0]
        for j in (1, 2):
            top = jnp.maximum(top, jnp.where(live[j], tops[j], -BIG))
        top = top * (SCALE * LOG2E)
        shifts = [top] + [jnp.where(live[j], top, BIG) for j in (1, 2)]
        powers = [jnp.exp2(s * (SCALE * LOG2E) - h) for s, h in zip(scores, shifts)]
        total = sum(jnp.sum(p, axis=0, keepdims=True) for p in powers)
        mixed = sum(jnp.sum(p * w, axis=0, keepdims=True) for p, w in zip(powers, weight_grads))
        inverse = 1.0 / total
        delta = mixed * inverse
        weights = [p * inverse for p in powers]
        grads = [(p * (w - delta)).astype(LOW) for p, w in zip(weights, weight_grads)]
        query_grad = sum(dot(d, k, 0, 0) for d, k in zip(grads, ks))
        query_grads.append((query_grad * SCALE).astype(LOW))
        blank = jnp.zeros((BLK - seen, tile), LOW)
        for j in range(3):
            low = weights[j].astype(LOW)
            pad = j == 0 and seen < BLK
            weights_low[j].append(jnp.concatenate([low, blank], 0) if pad else low)
            score_grads[j].append(jnp.concatenate([grads[j], blank], 0) if pad else grads[j])
    key_grads = [dot(jnp.concatenate(d, 1), query, 1, 0) for d in score_grads]
    value_grads = [dot(jnp.concatenate(w, 1), grad, 1, 0) for w in weights_low]
    return jnp.concatenate(query_grads, 0), key_grads, value_grads


def attend_kernel(start, plan, query, grad, key0, value0, pick1, pick2, query_grad, own, picks, acc, sums):
    i = pl.program_id(0)

    @pl.when(i == 0)
    def _():
        sums[...] = jnp.zeros_like(sums)

    acc[...] = jnp.zeros_like(acc)
    live = (True, plan[start + 6 + 2 * i] == 1, plan[start + 7 + 2 * i] == 1)

    def body(h, _):
        columns = pl.ds(pl.multiple_of(h * HEAD, HEAD), HEAD)
        keys = [key0[...], pick1[0, 0], pick2[0, 0]]
        values = [value0[...], pick1[1, 0], pick2[1, 0]]
        part, key_grads, value_grads = head_step(
            query[:, columns], grad[:, columns], keys, values, live, 256
        )
        query_grad[:, columns] = part
        for j in range(3):
            acc[j, 0] += key_grads[j]
            acc[j, 1] += value_grads[j]
        return 0

    lax.fori_loop(0, query.shape[1] // HEAD, body, 0)
    for j in range(3):
        to = i if j == 0 else plan[start + 2 * i + j - 1]
        sums[to, 0] += acc[j, 0] * SCALE
        sums[to, 1] += acc[j, 1]

    @pl.when(i == 2)
    def _():
        for s in range(2):
            for t in range(3):
                own[s, t] = sums[t, s]
            for t in range(6):
                picks[s, t] = sums[3 + t, s].astype(LOW)


def attend(cap, plan, queries, out_grad, keys, values, fetched):
    start = layout(cap)["attend"]
    tile = (BLK, HEAD)
    rows = pl.BlockSpec((BLK, queries.shape[1]), lambda i, plan: (i, 0))
    own_rows = pl.BlockSpec(tile, lambda i, plan: (i, 0))
    grid_spec = pltpu.PrefetchScalarGridSpec(
        num_scalar_prefetch=1,
        grid=(3,),
        in_specs=[
            rows,
            rows,
            own_rows,
            own_rows,
            pl.BlockSpec((2, 1) + tile, lambda i, plan: (0, 2 * i, 0, 0)),
            pl.BlockSpec((2, 1) + tile, lambda i, plan: (0, 2 * i + 1, 0, 0)),
        ],
        out_specs=[
            rows,
            pl.BlockSpec((2, 3) + tile, lambda i, plan: (0, 0, 0, 0)),
            pl.BlockSpec((2, 6) + tile, lambda i, plan: (0, 0, 0, 0)),
        ],
        scratch_shapes=[pltpu.VMEM((3, 2) + tile, F32), pltpu.VMEM((9, 2) + tile, F32)],
    )
    return pl.pallas_call(
        functools.partial(attend_kernel, start),
        grid_spec=grid_spec,
        out_shape=[
            jax.ShapeDtypeStruct(queries.shape, LOW),
            jax.ShapeDtypeStruct((2, 3) + tile, F32),
            jax.ShapeDtypeStruct((2, 6) + tile, LOW),
        ],
        compiler_params=pltpu.CompilerParams(vmem_limit_bytes=VMEM_LIMIT),
        name="attend",
    )(plan, queries, out_grad, keys, values, fetched, fetched)


def give_back_kernel(
    cap, plan, query_grad, own, picks, query_out, key_out, value_out,
    parts, own_far, packed, came, to_first, from_first, home, done, landed,
    sends, recvs, query_sems, query_recvs, final_sends, final_recvs, local_sems,
):
    at = layout(cap)
    x, y, c, z = place()
    a, b = lines(x, y, c)
    sibling = (x * 8 + y * 2 + 1 - c, z)
    here = x * 8 + y * 2
    firsts = {o: on_first(x, y, c, z, o) for o in (1, 2, 3)}
    seconds = {o: on_second(x, y, c, z, o) for o in (1, 2, 3)}
    depth = {(k, o): (here + k, (z + o) % SIDE) for k in (0, 1) for o in (1, 2, 3)}
    greet(
        [sibling] + list(firsts.values()) + list(seconds.values()) + list(depth.values())
    )
    rows = query_out.shape[0]
    width = query_grad.shape[1]

    swap = remote(picks.at[1 - c], parts.at[pl.ds(6, 6)], sends, recvs, 0, sibling)
    swap.start()
    swap_own = remote(own.at[1 - c], own_far, sends, recvs, 1, sibling)
    swap_own.start()
    query_copies = []
    for o in (2, 1, 3):
        copy = remote(
            query_grad.at[pl.ds(((z + o) % SIDE) * rows, rows)],
            query_out.at[:, pl.ds(pl.multiple_of(z * width, HEAD), width)],
            query_sems,
            query_recvs,
            o - 1,
            (here + c, (z + o) % SIDE),
        )
        copy.start()
        query_copies.append(copy)
    stay = pltpu.make_async_copy(
        query_grad.at[pl.ds(z * rows, rows)],
        query_out.at[:, pl.ds(pl.multiple_of(z * width, HEAD), width)],
        local_sems.at[0],
    )
    stay.start()

    for t in range(6):
        parts[t] = picks[c, t]
    parts[12] = jnp.zeros((BLK, HEAD), LOW)
    came[3 * cap] = jnp.zeros((BLK, HEAD), LOW)
    swap.wait_recv()

    passes = []
    for o in (2, 1, 3):

        def pack(s, _):
            start = at["pack"] + 2 * ((o - 1) * cap + s)
            total = parts[plan[start]].astype(F32) + parts[plan[start + 1]].astype(F32)
            packed[(o - 1) * cap + s] = total.astype(LOW)
            return 0

        lax.fori_loop(0, cap, pack, 0)
        copy = remote(
            packed.at[pl.ds((o - 1) * cap, cap)],
            came.at[pl.ds((3 - o) * cap, cap)],
            sends,
            recvs,
            1 + o,
            seconds[o],
        )
        copy.start()
        passes.append(copy)
    for copy in passes:
        copy.wait_recv()

    def line_sum(t):
        start = at["acc"] + 5 * t
        total = came[plan[start]].astype(F32)
        for k in (1, 2):
            total += came[plan[start + k]].astype(F32)
        for k in (3, 4):
            total += parts[plan[start + k]].astype(F32)
        return total

    homeward = []
    for o in (2, 1, 3):
        line = (a + o) % SIDE

        def one(t, _):
            to_first[(o - 1) * ROW + t] = line_sum(line * ROW + t).astype(LOW)
            return 0

        lax.fori_loop(0, ROW, one, 0)
        copy = remote(
            to_first.at[pl.ds((o - 1) * ROW, ROW)],
            from_first.at[pl.ds((3 - o) * ROW, ROW)],
            sends,
            recvs,
            4 + o,
            firsts[o],
        )
        copy.start()
        homeward.append(copy)
    swap_own.wait_recv()

    def mine(t, _):
        home[c * 3 + t] = line_sum(a * ROW + c * 3 + t) + own[c, t]
        home[(1 - c) * 3 + t] = line_sum(a * ROW + (1 - c) * 3 + t) + own_far[t]
        return 0

    lax.fori_loop(0, 3, mine, 0)
    for copy in homeward:
        copy.wait_recv()

    finals = []
    columns = pl.ds(pl.multiple_of(z * HEAD, HEAD), HEAD)
    for k in (0, 1):

        def finish(t, _):
            total = home[k * 3 + t]
            for o in range(3):
                total += from_first[o * ROW + k * 3 + t].astype(F32)
            done[k, pl.ds(pl.multiple_of(t * BLK, BLK), BLK)] = total.astype(LOW)
            return 0

        lax.fori_loop(0, 3, finish, 0)
        for o in (2, 1, 3):
            copy = remote(
                done.at[k, pl.ds(((z + o) % SIDE) * rows, rows)],
                landed.at[c, :, columns],
                final_sends.at[k],
                final_recvs.at[c],
                o,
                depth[k, o],
            )
            copy.start()
            finals.append(copy)
    cross = remote(
        done.at[1 - c, pl.ds(z * rows, rows)],
        landed.at[c, :, columns],
        final_sends.at[1 - c],
        final_recvs.at[c],
        0,
        sibling,
    )
    cross.start()
    keep = pltpu.make_async_copy(
        done.at[c, pl.ds(z * rows, rows)], landed.at[c, :, columns], local_sems.at[1]
    )
    keep.start()
    keep.wait()
    for role in (0, 1):
        for o in (1, 2, 3):
            remote(
                done.at[0, pl.ds(0, rows)],
                landed.at[role, :, pl.ds(0, HEAD)],
                final_sends.at[0],
                final_recvs.at[role],
                o,
                sibling,
            ).wait_recv()
    remote(
        done.at[0, pl.ds(0, rows)],
        landed.at[1 - c, :, columns],
        final_sends.at[0],
        final_recvs.at[1 - c],
        0,
        sibling,
    ).wait_recv()
    key_out[...] = landed[0]
    value_out[...] = landed[1]
    for copy in query_copies:
        copy.wait()
    stay.wait()
    for copy in [swap, swap_own] + passes + homeward + finals + [cross]:
        copy.wait_send()


def give_back(cap, plan, query_grad, own, picks):
    vmem = pl.BlockSpec(memory_space=pltpu.VMEM)
    anywhere = pl.BlockSpec(memory_space=pl.ANY)
    tile = (BLK, HEAD)
    rows = query_grad.shape[0] // SIDE
    dma = pltpu.SemaphoreType.DMA
    return pl.pallas_call(
        functools.partial(give_back_kernel, cap),
        out_shape=[
            jax.ShapeDtypeStruct((rows, SIDE * query_grad.shape[1]), LOW),
            jax.ShapeDtypeStruct((rows, SIDE * HEAD), LOW),
            jax.ShapeDtypeStruct((rows, SIDE * HEAD), LOW),
        ],
        in_specs=[pl.BlockSpec(memory_space=pltpu.SMEM), anywhere, vmem, vmem],
        out_specs=[anywhere, vmem, vmem],
        scratch_shapes=[
            pltpu.VMEM((13,) + tile, LOW),
            pltpu.VMEM((3,) + tile, F32),
            pltpu.VMEM((3 * cap,) + tile, LOW),
            pltpu.VMEM((3 * cap + 1,) + tile, LOW),
            pltpu.VMEM((3 * ROW,) + tile, LOW),
            pltpu.VMEM((3 * ROW,) + tile, LOW),
            pltpu.VMEM((ROW,) + tile, F32),
            pltpu.VMEM((2, 3 * BLK, HEAD), LOW),
            pltpu.VMEM((2, rows, SIDE * HEAD), LOW),
            dma((8,)),
            dma((8,)),
            dma((3,)),
            dma((3,)),
            dma((2, 4)),
            dma((2, 4)),
            dma((2,)),
        ],
        compiler_params=pltpu.CompilerParams(
            collective_id=1, has_side_effects=True, vmem_limit_bytes=VMEM_LIMIT
        ),
        name="give_back",
    )(plan, query_grad, own, picks)


def per_device(queries, key_rows, value_rows, out_grad, picked):
    cap = 12
    plan = make_plan(cap, picked)
    fetched = fetch(cap, plan, key_rows, value_rows)
    query_grad, own, picks = attend(
        cap, plan, queries, out_grad, key_rows, value_rows, fetched
    )
    return tuple(give_back(cap, plan, query_grad, own, picks))


def solution(mesh):
    return jax.shard_map(
        per_device,
        mesh=mesh,
        in_specs=(P("ctx", "kvh"), P("ctx", "kvh"), P("ctx", "kvh"), P("ctx", "kvh"), P()),
        out_specs=(P(("ctx", "kvh"), None), P(("ctx", "kvh"), None), P(("ctx", "kvh"), None)),
        check_vma=False,
    )
```

```python
import functools

import jax
import jax.numpy as jnp
from jax import lax
from jax.experimental import pallas as pl
from jax.experimental.pallas import tpu as pltpu
from jax.sharding import PartitionSpec as P

HEAD = 128
BLK = 512
SIDE = 4
ROW = 6
LINE = SIDE * ROW
SCALE = 1.0 / HEAD**0.5
LOG2E = 1.4426950408889634
BIG = 3.0e38
MESH = pl.DeviceIdType.MESH
F32 = jnp.float32
LOW = jnp.bfloat16
VMEM_LIMIT = 56 * 2**20


def place():
    index = lax.axis_index("ctx")
    x, y, c = index // 8, (index // 2) % 4, index % 2
    return x, y, c, lax.axis_index("kvh")


def lines(x, y, c):
    return x * (1 - c) + y * c, y * (1 - c) + x * c


def on_first(x, y, c, z, o):
    xx = (x + o * (1 - c)) % SIDE
    yy = (y + o * c) % SIDE
    return (xx * 8 + yy * 2 + c, z)


def on_second(x, y, c, z, o):
    xx = (x + o * c) % SIDE
    yy = (y + o * (1 - c)) % SIDE
    return (xx * 8 + yy * 2 + c, z)


def remote(src, dst, sends, recvs, k, device):
    return pltpu.make_async_remote_copy(
        src_ref=src,
        dst_ref=dst,
        send_sem=sends.at[k],
        recv_sem=recvs.at[k],
        device_id=device,
        device_id_type=MESH,
    )


def greet(devices):
    barrier = pltpu.get_barrier_semaphore()
    for device in devices:
        pl.semaphore_signal(barrier, inc=1, device_id=device, device_id_type=MESH)
    pl.semaphore_wait(barrier, len(devices))


def dot(left, right, left_dim, right_dim):
    return lax.dot_general(
        left, right, (((left_dim,), (right_dim,)), ((), ())), preferred_element_type=F32
    )


def head_step(query, grad, keys, values, live, tile):
    weights_low = [[], [], []]
    score_grads = [[], [], []]
    query_grads = []
    for r in range(BLK // tile):
        rows = slice(r * tile, (r + 1) * tile)
        seen = (r + 1) * tile
        ks = [keys[0][:seen], keys[1], keys[2]]
        vs = [values[0][:seen], values[1], values[2]]
        scores = [dot(k, query[rows], 1, 1) for k in ks]
        key_at = lax.broadcasted_iota(jnp.int32, (tile, tile), 0)
        row_at = lax.broadcasted_iota(jnp.int32, (tile, tile), 1)
        corner = jnp.where(key_at <= row_at, scores[0][seen - tile :], -BIG)
        scores[0] = corner if r == 0 else jnp.concatenate([scores[0][: seen - tile], corner], 0)
        weight_grads = [dot(v, grad[rows], 1, 1) for v in vs]
        tops = [jnp.max(s, axis=0, keepdims=True) for s in scores]
        top = tops[0]
        for j in (1, 2):
            top = jnp.maximum(top, jnp.where(live[j], tops[j], -BIG))
        top = top * (SCALE * LOG2E)
        shifts = [top] + [jnp.where(live[j], top, BIG) for j in (1, 2)]
        powers = [jnp.exp2(s * (SCALE * LOG2E) - h) for s, h in zip(scores, shifts)]
        total = sum(jnp.sum(p, axis=0, keepdims=True) for p in powers)
        mixed = sum(jnp.sum(p * w, axis=0, keepdims=True) for p, w in zip(powers, weight_grads))
        inverse = 1.0 / total
        delta = mixed * inverse
        weights = [p * inverse for p in powers]
        grads = [(p * (w - delta)).astype(LOW) for p, w in zip(weights, weight_grads)]
        query_grad = sum(dot(d, k, 0, 0) for d, k in zip(grads, ks))
        query_grads.append((query_grad * SCALE).astype(LOW))
        blank = jnp.zeros((BLK - seen, tile), LOW)
        for j in range(3):
            low = weights[j].astype(LOW)
            pad = j == 0 and seen < BLK
            weights_low[j].append(jnp.concatenate([low, blank], 0) if pad else low)
            score_grads[j].append(jnp.concatenate([grads[j], blank], 0) if pad else grads[j])
    key_grads = [dot(jnp.concatenate(d, 1), query, 1, 0) for d in score_grads]
    value_grads = [dot(jnp.concatenate(w, 1), grad, 1, 0) for w in weights_low]
    return jnp.concatenate(query_grads, 0), key_grads, value_grads


def second_of(block, c):
    return ((block // ROW) % 4) * (1 - c) + (block // LINE) * c


def near_at(block, c):
    first = (block // LINE) * (1 - c) + ((block // ROW) % 4) * c
    return first * ROW + block % ROW


def kernel(
    picked, queries, keys, values, out_grad, query_out, key_out, value_out,
    query_v, grad_v, query_grad, pair, near, give, chosen, acc, own, own_far, other_part,
    sums, to_first, from_first, home, done, landed, at_home,
    sends, recvs, query_sems, query_recvs, final_sends, final_recvs, local_sems,
    *rounds,
):
    packed, far, parts, merged, came = (rounds[3 * k : 3 * k + 3] for k in range(5))
    x, y, c, z = place()
    a, b = lines(x, y, c)
    index = x * 8 + y * 2 + c
    chip = x * 4 + y
    here = x * 8 + y * 2
    sibling = (here + 1 - c, z)
    firsts = {o: on_first(x, y, c, z, o) for o in (1, 2, 3)}
    seconds = {o: on_second(x, y, c, z, o) for o in (1, 2, 3)}
    depth = {(k, o): (here + k, (z + o) % SIDE) for k in (0, 1) for o in (1, 2, 3)}
    up, down = firsts[1], firsts[3]

    loads = [
        pltpu.make_async_copy(queries, query_v, local_sems.at[2]),
        pltpu.make_async_copy(out_grad, grad_v, local_sems.at[3]),
    ]
    for load in loads:
        load.start()
    for t in range(3):
        pair[0, t] = keys[t * BLK : (t + 1) * BLK]
        pair[1, t] = values[t * BLK : (t + 1) * BLK]
    for t in range(3):
        near[a * ROW + c * 3 + t] = pair[c, t]
    greet([sibling, up, down, seconds[1], seconds[3]] + list(depth.values()))

    mine = near.at[pl.ds(a * ROW + c * 3, 3)]
    theirs = near.at[pl.ds(a * ROW + (1 - c) * 3, 3)]
    swap = remote(pair.at[1 - c], near.at[pl.ds(b * ROW + c * 3, 3)], sends, recvs, 0, sibling)
    swap.start()
    copies = [
        remote(mine, mine, sends, recvs, 1, up),
        remote(mine, mine, sends, recvs, 2, down),
    ]
    copies[0].start()
    copies[1].start()
    swap.wait_recv()
    copies += [
        remote(theirs, theirs, sends, recvs, 3, up),
        remote(theirs, theirs, sends, recvs, 4, down),
    ]
    copies[3].start()
    copies[2].start()
    copies[0].wait_recv()
    below = near.at[pl.ds(((a + 3) % 4) * ROW + c * 3, 3)]
    copies.append(remote(below, below, sends, recvs, 5, up))
    copies[4].start()
    copies[3].wait_recv()
    above = near.at[pl.ds(((a + 1) % 4) * ROW + (1 - c) * 3, 3)]
    copies.append(remote(above, above, sends, recvs, 6, down))
    copies[5].start()

    def chip_at(o):
        other = (b + o) % SIDE
        return (x * 4 + other) * (1 - c) + (other * 4 + y) * c

    def pick_of(of_chip, r, s):
        return picked[(of_chip * ROW + (s // 2) * 3 + r) * 2 + s % 2]

    for r in range(3):
        for o in range(4):
            line_chip = chip_at(o)
            blocks = [pick_of(line_chip, r, s) for s in range(4)]
            for s in range(4):
                known = second_of(blocks[s], c) == b
                if s >= 2:
                    again = jnp.logical_or(blocks[s] == blocks[0], blocks[s] == blocks[1])
                    known = jnp.logical_and(known, jnp.logical_not(again))
                at_home[(r * 4 + o) * 4 + s] = jnp.where(known, near_at(blocks[s], c), -1)
    for k in (1, 2, 4, 5):
        copies[k].wait_recv()

    above2, below2 = seconds[1], seconds[3]

    def flow(r, m):
        place_at = pl.ds(2 * m, 2)
        target = below2 if m in (1, 4, 5) else above2
        return remote(packed[r].at[place_at], far[r].at[place_at], sends, recvs, 7 + 6 * r + m, target)

    def served(r, o, k):
        block = pick_of(chip_at(o), r, k)
        hit = second_of(block, c) == b
        return hit, near[jnp.where(hit, near_at(block, c), 0)]

    def send_round(r):
        for m, o, first in ((0, 2, 2), (1, 2, 0), (2, 1, 0), (5, 3, 2)):
            for k in range(2):
                packed[r][2 * m + k] = served(r, o, first + k)[1]
            flow(r, m).start()

    def relay_round(r):
        for m, o, first in ((3, 1, 2), (4, 3, 0)):
            flow(r, m - 3).wait_recv()
            for k in range(2):
                hit, block = served(r, o, first + k)
                packed[r][2 * m + k] = jnp.where(hit, block, far[r][2 * (m - 3) + k])
            flow(r, m).start()

    def chosen_copy(r):
        return remote(
            give.at[pl.ds(2 * r, 2)], chosen.at[pl.ds(4 * r + 2 * c, 2)], sends, recvs, 25 + r, sibling
        )

    def take_round(r):
        for m in (2, 3, 4, 5):
            flow(r, m).wait_recv()

        def pick(core, j):
            k = core * 2 + j
            block = pick_of(chip, r, k)
            o = (second_of(block, c) - b + 4) % 4
            over = jnp.logical_or(o == 1, jnp.logical_and(o == 2, k < 2))
            from_far = far[r][jnp.where(over, 8 + k, 4 + k)]
            return jnp.where(o > 0, from_far, near[near_at(block, c)])

        for j in range(2):
            give[2 * r + j] = pick(1 - c, j)
        chosen_copy(r).start()
        for j in range(2):
            chosen[4 * r + 2 * c + j] = pick(c, j)

    def part_copy(r):
        return remote(
            other_part.at[pl.ds(2 * r, 2)], parts[r].at[pl.ds(2 * c, 2)], sends, recvs, 28 + r, sibling
        )

    def give_round(r):
        for j in range(2):
            for role in range(2):
                value = acc[1 + j, role] * SCALE if role == 0 else acc[1 + j, role]
                low = value.astype(LOW)

                @pl.when(c == role)
                def _():
                    parts[r][2 * c + j] = low

                @pl.when(c != role)
                def _():
                    other_part[2 * r + j] = low

        part_copy(r).start()

    def back_flow(r, m):
        source, start, at, target = (
            (merged[r], 0, 8, above2),
            (merged[r], 2, 10, above2),
            (merged[r], 2, 2, below2),
            (merged[r], 0, 0, below2),
            (came[r], 8, 4, above2),
            (came[r], 2, 6, below2),
        )[m]
        return remote(
            source.at[pl.ds(start, 2)], came[r].at[pl.ds(at, 2)], sends, recvs, 31 + 6 * r + m, target
        )

    def back_round(r):
        part_copy(r).wait_recv()
        blocks = [pick_of(chip, r, s) for s in range(4)]
        for s in range(2):
            same = [blocks[k] == blocks[s] for k in (2, 3)]
            if s == 1:
                same = [jnp.logical_and(k, blocks[0] != blocks[1]) for k in same]
            extra = parts[r][jnp.where(same[0], 2, jnp.where(same[1], 3, 4))]
            merged[r][s] = (parts[r][s].astype(F32) + extra.astype(F32)).astype(LOW)
        for s in (2, 3):
            merged[r][s] = parts[r][s]
        for m in (0, 2, 1, 3):
            back_flow(r, m).start()

    def back_relay(r):
        for m in (0, 2):
            back_flow(r, m).wait_recv()
            back_flow(r, 4 + m // 2).start()

    send_round(0)
    blank = jnp.zeros((BLK, HEAD), LOW)
    for r in range(3):
        parts[r][4] = blank
        merged[r][4] = blank
        came[r][12] = blank
    for load in loads:
        load.wait()
    relay_round(0)
    take_round(0)
    chosen_copy(0).wait_recv()

    for r in range(3):
        if r < 2:
            send_round(r + 1)
        acc[...] = jnp.zeros_like(acc)
        rows = pl.ds(r * BLK, BLK)
        block = index * 3 + r
        live = (True, picked[2 * block] != block, picked[2 * block + 1] != block)

        def body(h, _):
            @pl.when(h == 1)
            def _():
                if r < 2:
                    relay_round(r + 1)
                if r > 0:
                    back_round(r - 1)

            @pl.when(h == 2)
            def _():
                if r > 0:
                    back_relay(r - 1)

            @pl.when(h == 3)
            def _():
                if r < 2:
                    take_round(r + 1)

            columns = pl.ds(pl.multiple_of(h * HEAD, HEAD), HEAD)
            key_tiles = [keys[rows], chosen[4 * r], chosen[4 * r + 1]]
            value_tiles = [values[rows], chosen[4 * r + 2], chosen[4 * r + 3]]
            part, key_grads, value_grads = head_step(
                query_v[rows, columns], grad_v[rows, columns], key_tiles, value_tiles, live, 256
            )
            query_grad[rows, columns] = part
            for j in range(3):
                acc[j, 0] += key_grads[j]
                acc[j, 1] += value_grads[j]
            return 0

        lax.fori_loop(0, 4, body, 0)
        own[0, r] = acc[0, 0] * SCALE
        own[1, r] = acc[0, 1]
        give_round(r)
        if r < 2:
            chosen_copy(r + 1).wait_recv()

    swap_own = remote(own.at[1 - c], own_far, sends, recvs, 49, sibling)
    swap_own.start()
    height = query_out.shape[0]
    width = query_grad.shape[1]
    query_columns = pl.ds(pl.multiple_of(z * width, HEAD), width)
    back_round(2)
    query_copies = []
    for o in (2, 1, 3):
        copy = remote(
            query_grad.at[pl.ds(((z + o) % SIDE) * height, height)],
            query_out.at[:, query_columns],
            query_sems,
            query_recvs,
            o - 1,
            (index, (z + o) % SIDE),
        )
        copy.start()
        query_copies.append(copy)
    stay = pltpu.make_async_copy(
        query_grad.at[pl.ds(z * height, height)], query_out.at[:, query_columns], local_sems.at[0]
    )
    stay.start()

    def round_sum(r, t):
        total = None
        for o in range(4):
            start = (r * 4 + o) * 4
            base = max(o - 1, 0) * 4
            spot = 4 if o == 0 else 12
            for s in (3, 2, 1, 0):
                spot = jnp.where(at_home[start + s] == t, base + s, spot)
            value = (merged[r] if o == 0 else came[r])[spot].astype(F32)
            total = value if total is None else total + value
        return total

    for r in (0, 1):
        for m in (1, 3, 4, 5):
            back_flow(r, m).wait_recv()

    def early(t, _):
        sums[t] = round_sum(0, t) + round_sum(1, t)
        return 0

    lax.fori_loop(0, LINE // 2, early, 0)
    back_relay(2)
    lax.fori_loop(LINE // 2, LINE, early, 0)
    swap_own.wait_recv()

    def add_own(t, _):
        sums[a * ROW + c * 3 + t] += own[c, t]
        sums[a * ROW + (1 - c) * 3 + t] += own_far[t]
        return 0

    lax.fori_loop(0, 3, add_own, 0)
    for m in (1, 3, 4, 5):
        back_flow(2, m).wait_recv()

    def homeward(m):
        place_at = pl.ds(3 * m, 3)
        target = down if m in (1, 2, 5) else up
        return remote(to_first.at[place_at], from_first.at[place_at], sends, recvs, 50 + m, target)

    for m, o, core in ((0, 2, 0), (2, 3, 0), (1, 2, 1), (3, 1, 1)):
        start = ((a + o) % SIDE) * ROW + core * 3

        def one(t, _):
            to_first[3 * m + t] = (sums[start + t] + round_sum(2, start + t)).astype(LOW)
            return 0

        lax.fori_loop(0, 3, one, 0)
        homeward(m).start()
    for m, o, core in ((4, 1, 0), (5, 3, 1)):
        start = ((a + o) % SIDE) * ROW + core * 3

        def ready(t, _):
            sums[start + t] += round_sum(2, start + t)
            return 0

        def one(t, _):
            to_first[3 * m + t] = (sums[start + t] + from_first[3 * (m - 4) + t].astype(F32)).astype(LOW)
            return 0

        lax.fori_loop(0, 3, ready, 0)
        homeward(m - 4).wait_recv()
        lax.fori_loop(0, 3, one, 0)
        homeward(m).start()

    def stays(t, _):
        home[t] = sums[a * ROW + t] + round_sum(2, a * ROW + t)
        return 0

    lax.fori_loop(0, ROW, stays, 0)

    finals = []
    columns = pl.ds(pl.multiple_of(z * HEAD, HEAD), HEAD)
    for k in (0, 1):
        for m in (2 + k, 4 + k):
            homeward(m).wait_recv()

        def finish(t, _):
            total = home[k * 3 + t]
            for m in (2 + k, 4 + k):
                total += from_first[3 * m + t].astype(F32)
            done[k, pl.ds(pl.multiple_of(t * BLK, BLK), BLK)] = total.astype(LOW)
            return 0

        lax.fori_loop(0, 3, finish, 0)
        for o in (2, 1, 3):
            copy = remote(
                done.at[k, pl.ds(((z + o) % SIDE) * height, height)],
                landed.at[c, :, columns],
                final_sends.at[k],
                final_recvs.at[c],
                o,
                depth[k, o],
            )
            copy.start()
            finals.append(copy)
    cross = remote(
        done.at[1 - c, pl.ds(z * height, height)],
        landed.at[c, :, columns],
        final_sends.at[1 - c],
        final_recvs.at[c],
        0,
        sibling,
    )
    cross.start()
    keep = pltpu.make_async_copy(
        done.at[c, pl.ds(z * height, height)], landed.at[c, :, columns], local_sems.at[1]
    )
    keep.start()
    keep.wait()
    for role in (0, 1):
        for o in (1, 2, 3):
            remote(
                done.at[0, pl.ds(0, height)],
                landed.at[role, :, pl.ds(0, HEAD)],
                final_sends.at[0],
                final_recvs.at[role],
                o,
                sibling,
            ).wait_recv()
    remote(
        done.at[0, pl.ds(0, height)],
        landed.at[1 - c, :, columns],
        final_sends.at[0],
        final_recvs.at[1 - c],
        0,
        sibling,
    ).wait_recv()
    key_out[...] = landed[0]
    value_out[...] = landed[1]
    for copy in query_copies:
        copy.wait()
    stay.wait()
    ends = [swap, swap_own] + copies + finals + [cross] + [homeward(m) for m in range(6)]
    for r in range(3):
        ends += [chosen_copy(r), part_copy(r)]
        ends += [flow(r, m) for m in range(6)] + [back_flow(r, m) for m in range(6)]
    for copy in ends:
        copy.wait_send()


def per_device(queries, key_rows, value_rows, out_grad, picked):
    vmem = pl.BlockSpec(memory_space=pltpu.VMEM)
    anywhere = pl.BlockSpec(memory_space=pl.ANY)
    tile = (BLK, HEAD)
    tokens, width = queries.shape
    height = tokens // SIDE
    dma = pltpu.SemaphoreType.DMA

    def blocks(count, kind=LOW):
        return pltpu.VMEM((count,) + tile, kind)

    return tuple(
        pl.pallas_call(
            kernel,
            out_shape=[
                jax.ShapeDtypeStruct((height, SIDE * width), LOW),
                jax.ShapeDtypeStruct((height, SIDE * HEAD), LOW),
                jax.ShapeDtypeStruct((height, SIDE * HEAD), LOW),
            ],
            in_specs=[pl.BlockSpec(memory_space=pltpu.SMEM), anywhere, vmem, vmem, anywhere],
            out_specs=[anywhere, vmem, vmem],
            scratch_shapes=[
                pltpu.VMEM((tokens, width), LOW),
                pltpu.VMEM((tokens, width), LOW),
                pltpu.VMEM((tokens, width), LOW),
                pltpu.VMEM((2, 3) + tile, LOW),
                blocks(LINE),
                blocks(6),
                blocks(12),
                pltpu.VMEM((3, 2) + tile, F32),
                pltpu.VMEM((2, 3) + tile, F32),
                blocks(3, F32),
                blocks(6),
                blocks(LINE, F32),
                blocks(3 * ROW),
                blocks(3 * ROW),
                blocks(ROW, F32),
                pltpu.VMEM((2, 3 * BLK, HEAD), LOW),
                pltpu.VMEM((2, height, SIDE * HEAD), LOW),
                pltpu.SMEM((48,), jnp.int32),
                dma((56,)),
                dma((56,)),
                dma((3,)),
                dma((3,)),
                dma((2, 4)),
                dma((2, 4)),
                dma((4,)),
            ]
            + [blocks(12)] * 6
            + [blocks(5)] * 6
            + [blocks(13)] * 3,
            compiler_params=pltpu.CompilerParams(
                collective_id=0, has_side_effects=True, vmem_limit_bytes=VMEM_LIMIT
            ),
            name="attend",
        )(picked.reshape(-1), queries, key_rows, value_rows, out_grad)
    )


def solution(mesh):
    return jax.shard_map(
        per_device,
        mesh=mesh,
        in_specs=(P("ctx", "kvh"), P("ctx", "kvh"), P("ctx", "kvh"), P("ctx", "kvh"), P()),
        out_specs=(P(("ctx", "kvh"), None), P(("ctx", "kvh"), None), P(("ctx", "kvh"), None)),
        check_vma=False,
    )
```

```python
import functools

import jax
import jax.numpy as jnp
from jax import lax
from jax.experimental import pallas as pl
from jax.experimental.pallas import tpu as pltpu
from jax.sharding import PartitionSpec as P

HEAD = 128
BLK = 512
SIDE = 4
ROW = 6
LINE = SIDE * ROW
SCALE = 1.0 / HEAD**0.5
LOG2E = 1.4426950408889634
BIG = 3.0e38
MESH = pl.DeviceIdType.MESH
F32 = jnp.float32
LOW = jnp.bfloat16
VMEM_LIMIT = 56 * 2**20


def place():
    index = lax.axis_index("ctx")
    x, y, c = index // 8, (index // 2) % 4, index % 2
    return x, y, c, lax.axis_index("kvh")


def lines(x, y, c):
    return x * (1 - c) + y * c, y * (1 - c) + x * c


def on_first(x, y, c, z, o):
    xx = (x + o * (1 - c)) % SIDE
    yy = (y + o * c) % SIDE
    return (xx * 8 + yy * 2 + c, z)


def on_second(x, y, c, z, o):
    xx = (x + o * c) % SIDE
    yy = (y + o * (1 - c)) % SIDE
    return (xx * 8 + yy * 2 + c, z)


def remote(src, dst, sends, recvs, k, device):
    return pltpu.make_async_remote_copy(
        src_ref=src,
        dst_ref=dst,
        send_sem=sends.at[k],
        recv_sem=recvs.at[k],
        device_id=device,
        device_id_type=MESH,
    )


def greet(devices):
    barrier = pltpu.get_barrier_semaphore()
    for device in devices:
        pl.semaphore_signal(barrier, inc=1, device_id=device, device_id_type=MESH)
    pl.semaphore_wait(barrier, len(devices))


def dot(left, right, left_dim, right_dim):
    return lax.dot_general(
        left, right, (((left_dim,), (right_dim,)), ((), ())), preferred_element_type=F32
    )


TILE = 256
LOG_SCALE = SCALE * LOG2E


def corner_scores(key, query, seen):
    scores = dot(key[:seen], query, 1, 1)
    key_at = lax.broadcasted_iota(jnp.int32, (TILE, TILE), 0)
    row_at = lax.broadcasted_iota(jnp.int32, (TILE, TILE), 1)
    corner = jnp.where(key_at <= row_at, scores[seen - TILE :], -BIG)
    return corner if seen == TILE else jnp.concatenate([scores[: seen - TILE], corner], 0)


def column_sum(values):
    return jnp.sum(values, axis=0, keepdims=True)


def own_totals(query, grad, key, value, stats, k):
    for r in range(BLK // TILE):
        rows = slice(r * TILE, (r + 1) * TILE)
        seen = (r + 1) * TILE
        scores = corner_scores(key, query[rows], seen)
        weight_grads = dot(value[:seen], grad[rows], 1, 1)
        top = jnp.max(scores, axis=0, keepdims=True) * LOG_SCALE
        powers = jnp.exp2(scores * LOG_SCALE - top)
        stats[k, 0:1, rows] = top
        stats[k, 1:2, rows] = column_sum(powers)
        stats[k, 2:3, rows] = column_sum(powers * weight_grads)


def pick_step(query, grad, keys, values, live, stats, k):
    weights_low = [[], []]
    score_grads = [[], []]
    query_grads = []
    for r in range(BLK // TILE):
        rows = slice(r * TILE, (r + 1) * TILE)
        scores = [dot(key, query[rows], 1, 1) for key in keys]
        weight_grads = [dot(value, grad[rows], 1, 1) for value in values]
        own_top = stats[k, 0:1, rows]
        top = own_top
        for j in range(2):
            pick_top = jnp.max(scores[j], axis=0, keepdims=True) * LOG_SCALE
            top = jnp.maximum(top, jnp.where(live[j], pick_top, -BIG))
        shifts = [jnp.where(live[j], top, BIG) for j in range(2)]
        powers = [jnp.exp2(s * LOG_SCALE - h) for s, h in zip(scores, shifts)]
        own_part = jnp.exp2(own_top - top)
        total = stats[k, 1:2, rows] * own_part + column_sum(powers[0]) + column_sum(powers[1])
        mixed = stats[k, 2:3, rows] * own_part
        for p, w in zip(powers, weight_grads):
            mixed += column_sum(p * w)
        inverse = 1.0 / total
        delta = mixed * inverse
        stats[k, 0:1, rows] = top
        stats[k, 1:2, rows] = inverse
        stats[k, 2:3, rows] = delta
        weights = [p * inverse for p in powers]
        grads = [(p * (w - delta)).astype(LOW) for p, w in zip(weights, weight_grads)]
        query_grads.append(dot(grads[0], keys[0], 0, 0) + dot(grads[1], keys[1], 0, 0))
        for j in range(2):
            weights_low[j].append(weights[j].astype(LOW))
            score_grads[j].append(grads[j])
    key_grads = [dot(jnp.concatenate(d, 1), query, 1, 0) for d in score_grads]
    value_grads = [dot(jnp.concatenate(w, 1), grad, 1, 0) for w in weights_low]
    return jnp.concatenate(query_grads, 0), key_grads, value_grads


def own_step(query, grad, key, value, query_part, stats, k):
    weights_low = []
    score_grads = []
    query_grads = []
    for r in range(BLK // TILE):
        rows = slice(r * TILE, (r + 1) * TILE)
        seen = (r + 1) * TILE
        scores = corner_scores(key, query[rows], seen)
        weight_grads = dot(value[:seen], grad[rows], 1, 1)
        weights = jnp.exp2(scores * LOG_SCALE - stats[k, 0:1, rows]) * stats[k, 1:2, rows]
        low = weights.astype(LOW)
        grads = (weights * (weight_grads - stats[k, 2:3, rows])).astype(LOW)
        query_grads.append(((query_part[rows] + dot(grads, key[:seen], 0, 0)) * SCALE).astype(LOW))
        if seen < BLK:
            blank = jnp.zeros((BLK - seen, TILE), LOW)
            low = jnp.concatenate([low, blank], 0)
            grads = jnp.concatenate([grads, blank], 0)
        weights_low.append(low)
        score_grads.append(grads)
    key_grad = dot(jnp.concatenate(score_grads, 1), query, 1, 0)
    value_grad = dot(jnp.concatenate(weights_low, 1), grad, 1, 0)
    return jnp.concatenate(query_grads, 0), key_grad, value_grad


def second_of(block, c):
    return ((block // ROW) % 4) * (1 - c) + (block // LINE) * c


def near_at(block, c):
    first = (block // LINE) * (1 - c) + ((block // ROW) % 4) * c
    return first * ROW + block % ROW


def kernel(
    picked, queries, keys, values, out_grad, query_out, key_out, value_out,
    query_v, grad_v, query_grad, query_part, stats, pair, near, give, chosen, acc, own, own_far, other_part,
    sums, to_first, from_first, home, done, landed, at_home,
    sends, recvs, query_sems, query_recvs, final_sends, final_recvs, local_sems,
    *rounds,
):
    packed, far, parts, merged, came = (rounds[3 * k : 3 * k + 3] for k in range(5))
    x, y, c, z = place()
    a, b = lines(x, y, c)
    index = x * 8 + y * 2 + c
    chip = x * 4 + y
    here = x * 8 + y * 2
    sibling = (here + 1 - c, z)
    firsts = {o: on_first(x, y, c, z, o) for o in (1, 2, 3)}
    seconds = {o: on_second(x, y, c, z, o) for o in (1, 2, 3)}
    depth = {(k, o): (here + k, (z + o) % SIDE) for k in (0, 1) for o in (1, 2, 3)}
    up, down = firsts[1], firsts[3]

    loads = [
        pltpu.make_async_copy(queries, query_v, local_sems.at[2]),
        pltpu.make_async_copy(out_grad, grad_v, local_sems.at[3]),
    ]
    for load in loads:
        load.start()
    for t in range(3):
        pair[0, t] = keys[t * BLK : (t + 1) * BLK]
        pair[1, t] = values[t * BLK : (t + 1) * BLK]
    for t in range(3):
        near[a * ROW + c * 3 + t] = pair[c, t]
    greet([sibling, up, down, seconds[1], seconds[3]] + list(depth.values()))

    mine = near.at[pl.ds(a * ROW + c * 3, 3)]
    theirs = near.at[pl.ds(a * ROW + (1 - c) * 3, 3)]
    swap = remote(pair.at[1 - c], near.at[pl.ds(b * ROW + c * 3, 3)], sends, recvs, 0, sibling)
    swap.start()
    copies = [
        remote(mine, mine, sends, recvs, 1, up),
        remote(mine, mine, sends, recvs, 2, down),
    ]
    copies[0].start()
    copies[1].start()
    swap.wait_recv()
    copies += [
        remote(theirs, theirs, sends, recvs, 3, up),
        remote(theirs, theirs, sends, recvs, 4, down),
    ]
    copies[3].start()
    copies[2].start()

    def spots(r, h):
        rows = pl.ds(pl.multiple_of(r * BLK, BLK), BLK)
        return rows, pl.ds(pl.multiple_of(h * HEAD, HEAD), HEAD)

    def totals(k, _):
        rows, columns = spots(k // 4, k % 4)
        own_totals(query_v[rows, columns], grad_v[rows, columns], keys[rows], values[rows], stats, k)
        return 0

    for load in loads:
        load.wait()
    lax.fori_loop(0, 4, totals, 0)
    copies[0].wait_recv()
    below = near.at[pl.ds(((a + 3) % 4) * ROW + c * 3, 3)]
    copies.append(remote(below, below, sends, recvs, 5, up))
    copies[4].start()
    copies[3].wait_recv()
    above = near.at[pl.ds(((a + 1) % 4) * ROW + (1 - c) * 3, 3)]
    copies.append(remote(above, above, sends, recvs, 6, down))
    copies[5].start()

    def chip_at(o):
        other = (b + o) % SIDE
        return (x * 4 + other) * (1 - c) + (other * 4 + y) * c

    def pick_of(of_chip, r, s):
        return picked[(of_chip * ROW + (s // 2) * 3 + r) * 2 + s % 2]

    for r in range(3):
        for o in range(4):
            line_chip = chip_at(o)
            blocks = [pick_of(line_chip, r, s) for s in range(4)]
            for s in range(4):
                known = second_of(blocks[s], c) == b
                if s >= 2:
                    again = jnp.logical_or(blocks[s] == blocks[0], blocks[s] == blocks[1])
                    known = jnp.logical_and(known, jnp.logical_not(again))
                at_home[(r * 4 + o) * 4 + s] = jnp.where(known, near_at(blocks[s], c), -1)
    lax.fori_loop(4, 12, totals, 0)
    for k in (1, 2, 4, 5):
        copies[k].wait_recv()

    above2, below2 = seconds[1], seconds[3]

    def flow(r, m):
        place_at = pl.ds(2 * m, 2)
        target = below2 if m in (1, 4, 5) else above2
        return remote(packed[r].at[place_at], far[r].at[place_at], sends, recvs, 7 + 6 * r + m, target)

    def served(r, o, k):
        block = pick_of(chip_at(o), r, k)
        hit = second_of(block, c) == b
        return hit, near[jnp.where(hit, near_at(block, c), 0)]

    def send_round(r):
        for m, o, first in ((0, 2, 2), (1, 2, 0), (2, 1, 0), (5, 3, 2)):
            for k in range(2):
                packed[r][2 * m + k] = served(r, o, first + k)[1]
            flow(r, m).start()

    def relay_round(r):
        for m, o, first in ((3, 1, 2), (4, 3, 0)):
            flow(r, m - 3).wait_recv()
            for k in range(2):
                hit, block = served(r, o, first + k)
                packed[r][2 * m + k] = jnp.where(hit, block, far[r][2 * (m - 3) + k])
            flow(r, m).start()

    def chosen_copy(r):
        return remote(
            give.at[pl.ds(2 * r, 2)], chosen.at[pl.ds(4 * r + 2 * c, 2)], sends, recvs, 25 + r, sibling
        )

    def take_round(r):
        for m in (2, 3, 4, 5):
            flow(r, m).wait_recv()
        if r == 0:
            send_round(1)

        def pick(core, j):
            k = core * 2 + j
            block = pick_of(chip, r, k)
            o = (second_of(block, c) - b + 4) % 4
            over = jnp.logical_or(o == 1, jnp.logical_and(o == 2, k < 2))
            from_far = far[r][jnp.where(over, 8 + k, 4 + k)]
            return jnp.where(o > 0, from_far, near[near_at(block, c)])

        for j in range(2):
            give[2 * r + j] = pick(1 - c, j)
        chosen_copy(r).start()
        for j in range(2):
            chosen[4 * r + 2 * c + j] = pick(c, j)

    def part_copy(r):
        return remote(
            other_part.at[pl.ds(2 * r, 2)], parts[r].at[pl.ds(2 * c, 2)], sends, recvs, 28 + r, sibling
        )

    def give_round(r):
        for j in range(2):
            for role in range(2):
                value = acc[j, role] * SCALE if role == 0 else acc[j, role]
                low = value.astype(LOW)

                @pl.when(c == role)
                def _():
                    parts[r][2 * c + j] = low

                @pl.when(c != role)
                def _():
                    other_part[2 * r + j] = low

        part_copy(r).start()

    def back_flow(r, m):
        source, start, at, target = (
            (merged[r], 0, 8, above2),
            (merged[r], 2, 10, above2),
            (merged[r], 2, 2, below2),
            (merged[r], 0, 0, below2),
            (came[r], 8, 4, above2),
            (came[r], 2, 6, below2),
        )[m]
        return remote(
            source.at[pl.ds(start, 2)], came[r].at[pl.ds(at, 2)], sends, recvs, 31 + 6 * r + m, target
        )

    def back_round(r):
        part_copy(r).wait_recv()
        blocks = [pick_of(chip, r, s) for s in range(4)]
        for s in range(2):
            same = [blocks[k] == blocks[s] for k in (2, 3)]
            if s == 1:
                same = [jnp.logical_and(k, blocks[0] != blocks[1]) for k in same]
            extra = parts[r][jnp.where(same[0], 2, jnp.where(same[1], 3, 4))]
            merged[r][s] = (parts[r][s].astype(F32) + extra.astype(F32)).astype(LOW)
        for s in (2, 3):
            merged[r][s] = parts[r][s]
        for m in (0, 2, 1, 3):
            back_flow(r, m).start()

    def back_relay(r):
        for m in (0, 2):
            back_flow(r, m).wait_recv()
            back_flow(r, 4 + m // 2).start()

    send_round(0)
    blank = jnp.zeros((BLK, HEAD), LOW)
    for r in range(3):
        parts[r][4] = blank
        merged[r][4] = blank
        came[r][12] = blank
    relay_round(0)
    take_round(0)
    chosen_copy(0).wait_recv()

    for r in range(3):
        acc[...] = jnp.zeros_like(acc)
        rows = pl.ds(r * BLK, BLK)
        block = index * 3 + r
        live = (picked[2 * block] != block, picked[2 * block + 1] != block)

        def body(h, _):
            @pl.when(h == 1)
            def _():
                if r == 0:
                    relay_round(1)
                    send_round(2)
                if r > 0:
                    back_round(r - 1)

            @pl.when(h == 3)
            def _():
                if r < 2:
                    take_round(r + 1)
                if r > 0:
                    back_relay(r - 1)

            columns = pl.ds(pl.multiple_of(h * HEAD, HEAD), HEAD)
            part, key_grads, value_grads = pick_step(
                query_v[rows, columns],
                grad_v[rows, columns],
                [chosen[4 * r], chosen[4 * r + 1]],
                [chosen[4 * r + 2], chosen[4 * r + 3]],
                live,
                stats,
                4 * r + h,
            )
            query_part[rows, columns] = part
            for j in range(2):
                acc[j, 0] += key_grads[j]
                acc[j, 1] += value_grads[j]
            return 0

        if r == 1:
            relay_round(2)
        lax.fori_loop(0, 4, body, 0)
        give_round(r)
        if r < 2:
            chosen_copy(r + 1).wait_recv()

    height = query_out.shape[0]
    width = query_grad.shape[1]

    def query_copy(h, o):
        source = query_grad.at[pl.ds(((z + o) % SIDE) * height, height), spots(0, h)[1]]
        target = query_out.at[:, pl.ds(pl.multiple_of(z * width + h * HEAD, HEAD), HEAD)]
        if o == 0:
            return pltpu.make_async_copy(source, target, local_sems.at[4 + h])
        return remote(
            source, target, query_sems, query_recvs, 3 * h + o - 1, (index, (z + o) % SIDE)
        )

    own[...] = jnp.zeros_like(own)
    back_round(2)

    def round_sum(r, t):
        total = None
        for o in range(4):
            start = (r * 4 + o) * 4
            base = max(o - 1, 0) * 4
            spot = 4 if o == 0 else 12
            for s in (3, 2, 1, 0):
                spot = jnp.where(at_home[start + s] == t, base + s, spot)
            value = (merged[r] if o == 0 else came[r])[spot].astype(F32)
            total = value if total is None else total + value
        return total

    def early(t, _):
        sums[t] = round_sum(0, t) + round_sum(1, t)
        return 0

    def homeward(m):
        place_at = pl.ds(3 * m, 3)
        target = down if m in (1, 2, 5) else up
        return remote(to_first.at[place_at], from_first.at[place_at], sends, recvs, 50 + m, target)

    def send_home():
        for m in (1, 3, 4, 5):
            back_flow(2, m).wait_recv()
        for m, o, core in ((0, 2, 0), (2, 3, 0), (1, 2, 1), (3, 1, 1)):
            start = ((a + o) % SIDE) * ROW + core * 3

            def one(t, _):
                to_first[3 * m + t] = (sums[start + t] + round_sum(2, start + t)).astype(LOW)
                return 0

            lax.fori_loop(0, 3, one, 0)
            homeward(m).start()
        for o, core in ((1, 0), (3, 1)):
            start = ((a + o) % SIDE) * ROW + core * 3

            def ready(t, _):
                sums[start + t] += round_sum(2, start + t)
                return 0

            lax.fori_loop(0, 3, ready, 0)

    def relay_home():
        for m, o, core in ((4, 1, 0), (5, 3, 1)):
            start = ((a + o) % SIDE) * ROW + core * 3
            homeward(m - 4).wait_recv()

            def one(t, _):
                to_first[3 * m + t] = (sums[start + t] + from_first[3 * (m - 4) + t].astype(F32)).astype(LOW)
                return 0

            lax.fori_loop(0, 3, one, 0)
            homeward(m).start()

    def tail(h, _):
        @pl.when(h == 1)
        def _():
            back_relay(2)
            for r in (0, 1):
                for m in (1, 3, 4, 5):
                    back_flow(r, m).wait_recv()
            lax.fori_loop(0, LINE, early, 0)
            send_home()

        @pl.when(h == 3)
        def _():
            relay_home()

        def one(r, _):
            rows, columns = spots(r, h)
            low, key_grad, value_grad = own_step(
                query_v[rows, columns],
                grad_v[rows, columns],
                keys[rows],
                values[rows],
                query_part[rows, columns],
                stats,
                4 * r + h,
            )
            query_grad[rows, columns] = low
            own[0, r] += key_grad * SCALE
            own[1, r] += value_grad
            return 0

        lax.fori_loop(0, 3, one, 0)
        for o in (2, 1, 3, 0):
            query_copy(h, o).start()
        return 0

    lax.fori_loop(0, 4, tail, 0)
    swap_own = remote(own.at[1 - c], own_far, sends, recvs, 49, sibling)
    swap_own.start()

    def stays(t, _):
        home[t] = sums[a * ROW + t] + round_sum(2, a * ROW + t)
        return 0

    lax.fori_loop(0, ROW, stays, 0)
    swap_own.wait_recv()

    def add_own(t, _):
        home[c * 3 + t] += own[c, t]
        home[(1 - c) * 3 + t] += own_far[t]
        return 0

    lax.fori_loop(0, 3, add_own, 0)

    finals = []
    columns = pl.ds(pl.multiple_of(z * HEAD, HEAD), HEAD)
    for k in (0, 1):
        for m in (2 + k, 4 + k):
            homeward(m).wait_recv()

        def finish(t, _):
            total = home[k * 3 + t]
            for m in (2 + k, 4 + k):
                total += from_first[3 * m + t].astype(F32)
            done[k, pl.ds(pl.multiple_of(t * BLK, BLK), BLK)] = total.astype(LOW)
            return 0

        lax.fori_loop(0, 3, finish, 0)
        for o in (2, 1, 3):
            copy = remote(
                done.at[k, pl.ds(((z + o) % SIDE) * height, height)],
                landed.at[c, :, columns],
                final_sends.at[k],
                final_recvs.at[c],
                o,
                depth[k, o],
            )
            copy.start()
            finals.append(copy)
    cross = remote(
        done.at[1 - c, pl.ds(z * height, height)],
        landed.at[c, :, columns],
        final_sends.at[1 - c],
        final_recvs.at[c],
        0,
        sibling,
    )
    cross.start()
    keep = pltpu.make_async_copy(
        done.at[c, pl.ds(z * height, height)], landed.at[c, :, columns], local_sems.at[1]
    )
    keep.start()
    keep.wait()
    for role in (0, 1):
        for o in (1, 2, 3):
            remote(
                done.at[0, pl.ds(0, height)],
                landed.at[role, :, pl.ds(0, HEAD)],
                final_sends.at[0],
                final_recvs.at[role],
                o,
                sibling,
            ).wait_recv()
    remote(
        done.at[0, pl.ds(0, height)],
        landed.at[1 - c, :, columns],
        final_sends.at[0],
        final_recvs.at[1 - c],
        0,
        sibling,
    ).wait_recv()
    key_out[...] = landed[0]
    value_out[...] = landed[1]
    for h in range(4):
        for o in range(4):
            query_copy(h, o).wait()
    ends = [swap, swap_own] + copies + finals + [cross] + [homeward(m) for m in range(6)]
    for r in range(3):
        ends += [chosen_copy(r), part_copy(r)]
        ends += [flow(r, m) for m in range(6)] + [back_flow(r, m) for m in range(6)]
    for copy in ends:
        copy.wait_send()


def per_device(queries, key_rows, value_rows, out_grad, picked):
    vmem = pl.BlockSpec(memory_space=pltpu.VMEM)
    anywhere = pl.BlockSpec(memory_space=pl.ANY)
    tile = (BLK, HEAD)
    tokens, width = queries.shape
    height = tokens // SIDE
    dma = pltpu.SemaphoreType.DMA

    def blocks(count, kind=LOW):
        return pltpu.VMEM((count,) + tile, kind)

    return tuple(
        pl.pallas_call(
            kernel,
            out_shape=[
                jax.ShapeDtypeStruct((height, SIDE * width), LOW),
                jax.ShapeDtypeStruct((height, SIDE * HEAD), LOW),
                jax.ShapeDtypeStruct((height, SIDE * HEAD), LOW),
            ],
            in_specs=[pl.BlockSpec(memory_space=pltpu.SMEM), anywhere, vmem, vmem, anywhere],
            out_specs=[anywhere, vmem, vmem],
            scratch_shapes=[
                pltpu.VMEM((tokens, width), LOW),
                pltpu.VMEM((tokens, width), LOW),
                pltpu.VMEM((tokens, width), LOW),
                pltpu.VMEM((tokens, width), F32),
                pltpu.VMEM((12, 8, BLK), F32),
                pltpu.VMEM((2, 3) + tile, LOW),
                blocks(LINE),
                blocks(6),
                blocks(12),
                pltpu.VMEM((2, 2) + tile, F32),
                pltpu.VMEM((2, 3) + tile, F32),
                blocks(3, F32),
                blocks(6),
                blocks(LINE, F32),
                blocks(3 * ROW),
                blocks(3 * ROW),
                blocks(ROW, F32),
                pltpu.VMEM((2, 3 * BLK, HEAD), LOW),
                pltpu.VMEM((2, height, SIDE * HEAD), LOW),
                pltpu.SMEM((48,), jnp.int32),
                dma((56,)),
                dma((56,)),
                dma((12,)),
                dma((12,)),
                dma((2, 4)),
                dma((2, 4)),
                dma((8,)),
            ]
            + [blocks(12)] * 6
            + [blocks(5)] * 6
            + [blocks(13)] * 3,
            compiler_params=pltpu.CompilerParams(
                collective_id=0, has_side_effects=True, vmem_limit_bytes=VMEM_LIMIT
            ),
            name="attend",
        )(picked.reshape(-1), queries, key_rows, value_rows, out_grad)
    )


def solution(mesh):
    return jax.shard_map(
        per_device,
        mesh=mesh,
        in_specs=(P("ctx", "kvh"), P("ctx", "kvh"), P("ctx", "kvh"), P("ctx", "kvh"), P()),
        out_specs=(P(("ctx", "kvh"), None), P(("ctx", "kvh"), None), P(("ctx", "kvh"), None)),
        check_vma=False,
    )
```

```python
import functools

import jax
import jax.numpy as jnp
from jax import lax
from jax.experimental import pallas as pl
from jax.experimental.pallas import tpu as pltpu
from jax.sharding import PartitionSpec as P

HEAD = 128
BLK = 512
SIDE = 4
ROW = 6
LINE = SIDE * ROW
SCALE = 1.0 / HEAD**0.5
LOG2E = 1.4426950408889634
BIG = 3.0e38
MESH = pl.DeviceIdType.MESH
F32 = jnp.float32
LOW = jnp.bfloat16
VMEM_LIMIT = 56 * 2**20


def place():
    index = lax.axis_index("ctx")
    x, y, c = index // 8, (index // 2) % 4, index % 2
    return x, y, c, lax.axis_index("kvh")


def lines(x, y, c):
    return x * (1 - c) + y * c, y * (1 - c) + x * c


def on_first(x, y, c, z, o):
    xx = (x + o * (1 - c)) % SIDE
    yy = (y + o * c) % SIDE
    return (xx * 8 + yy * 2 + c, z)


def on_second(x, y, c, z, o):
    xx = (x + o * c) % SIDE
    yy = (y + o * (1 - c)) % SIDE
    return (xx * 8 + yy * 2 + c, z)


def remote(src, dst, sends, recvs, k, device):
    return pltpu.make_async_remote_copy(
        src_ref=src,
        dst_ref=dst,
        send_sem=sends.at[k],
        recv_sem=recvs.at[k],
        device_id=device,
        device_id_type=MESH,
    )


def greet(devices):
    barrier = pltpu.get_barrier_semaphore()
    for device in devices:
        pl.semaphore_signal(barrier, inc=1, device_id=device, device_id_type=MESH)
    return lambda: pl.semaphore_wait(barrier, len(devices))


def dot(left, right, left_dim, right_dim):
    return lax.dot_general(
        left, right, (((left_dim,), (right_dim,)), ((), ())), preferred_element_type=F32
    )


TILE = 256
LOG_SCALE = SCALE * LOG2E


def corner_scores(key, query, seen):
    scores = dot(key[:seen], query, 1, 1)
    key_at = lax.broadcasted_iota(jnp.int32, (TILE, TILE), 0)
    row_at = lax.broadcasted_iota(jnp.int32, (TILE, TILE), 1)
    corner = jnp.where(key_at <= row_at, scores[seen - TILE :], -BIG)
    return corner if seen == TILE else jnp.concatenate([scores[: seen - TILE], corner], 0)


def column_sum(values):
    return jnp.sum(values, axis=0, keepdims=True)


def own_totals(query, grad, key, value, stats, k):
    for r in range(BLK // TILE):
        rows = slice(r * TILE, (r + 1) * TILE)
        seen = (r + 1) * TILE
        scores = corner_scores(key, query[rows], seen)
        weight_grads = dot(value[:seen], grad[rows], 1, 1)
        top = jnp.max(scores, axis=0, keepdims=True) * LOG_SCALE
        powers = jnp.exp2(scores * LOG_SCALE - top)
        stats[k, 0:1, rows] = top
        stats[k, 1:2, rows] = column_sum(powers)
        stats[k, 2:3, rows] = column_sum(powers * weight_grads)


def pick_step(query, grad, keys, values, live, stats, k):
    weights_low = [[], []]
    score_grads = [[], []]
    query_grads = []
    for r in range(BLK // TILE):
        rows = slice(r * TILE, (r + 1) * TILE)
        scores = [dot(key, query[rows], 1, 1) for key in keys]
        weight_grads = [dot(value, grad[rows], 1, 1) for value in values]
        own_top = stats[k, 0:1, rows]
        top = own_top
        for j in range(2):
            pick_top = jnp.max(scores[j], axis=0, keepdims=True) * LOG_SCALE
            top = jnp.maximum(top, jnp.where(live[j], pick_top, -BIG))
        shifts = [jnp.where(live[j], top, BIG) for j in range(2)]
        powers = [jnp.exp2(s * LOG_SCALE - h) for s, h in zip(scores, shifts)]
        own_part = jnp.exp2(own_top - top)
        total = stats[k, 1:2, rows] * own_part + column_sum(powers[0]) + column_sum(powers[1])
        mixed = stats[k, 2:3, rows] * own_part
        for p, w in zip(powers, weight_grads):
            mixed += column_sum(p * w)
        inverse = 1.0 / total
        delta = mixed * inverse
        stats[k, 0:1, rows] = top
        stats[k, 1:2, rows] = inverse
        stats[k, 2:3, rows] = delta
        weights = [p * inverse for p in powers]
        grads = [(p * (w - delta)).astype(LOW) for p, w in zip(weights, weight_grads)]
        query_grads.append(dot(grads[0], keys[0], 0, 0) + dot(grads[1], keys[1], 0, 0))
        for j in range(2):
            weights_low[j].append(weights[j].astype(LOW))
            score_grads[j].append(grads[j])
    key_grads = [dot(jnp.concatenate(d, 1), query, 1, 0) for d in score_grads]
    value_grads = [dot(jnp.concatenate(w, 1), grad, 1, 0) for w in weights_low]
    return jnp.concatenate(query_grads, 0), key_grads, value_grads


def own_step(query, grad, key, value, query_part, stats, k):
    weights_low = []
    score_grads = []
    query_grads = []
    for r in range(BLK // TILE):
        rows = slice(r * TILE, (r + 1) * TILE)
        seen = (r + 1) * TILE
        scores = corner_scores(key, query[rows], seen)
        weight_grads = dot(value[:seen], grad[rows], 1, 1)
        weights = jnp.exp2(scores * LOG_SCALE - stats[k, 0:1, rows]) * stats[k, 1:2, rows]
        low = weights.astype(LOW)
        grads = (weights * (weight_grads - stats[k, 2:3, rows])).astype(LOW)
        query_grads.append(((query_part[rows] + dot(grads, key[:seen], 0, 0)) * SCALE).astype(LOW))
        if seen < BLK:
            blank = jnp.zeros((BLK - seen, TILE), LOW)
            low = jnp.concatenate([low, blank], 0)
            grads = jnp.concatenate([grads, blank], 0)
        weights_low.append(low)
        score_grads.append(grads)
    key_grad = dot(jnp.concatenate(score_grads, 1), query, 1, 0)
    value_grad = dot(jnp.concatenate(weights_low, 1), grad, 1, 0)
    return jnp.concatenate(query_grads, 0), key_grad, value_grad


def second_of(block, c):
    return ((block // ROW) % 4) * (1 - c) + (block // LINE) * c


def near_at(block, c):
    first = (block // LINE) * (1 - c) + ((block // ROW) % 4) * c
    return first * ROW + block % ROW


def kernel(
    picked, queries, keys, values, out_grad, query_out, key_out, value_out,
    query_v, grad_v, query_grad, query_part, stats, pair, near, give, chosen, acc, own, own_far, other_part,
    sums, to_first, from_first, home, done, landed, at_home,
    sends, recvs, query_sems, query_recvs, final_sends, final_recvs, local_sems,
    *rounds,
):
    packed, far, parts, merged, came = (rounds[3 * k : 3 * k + 3] for k in range(5))
    x, y, c, z = place()
    a, b = lines(x, y, c)
    index = x * 8 + y * 2 + c
    chip = x * 4 + y
    here = x * 8 + y * 2
    sibling = (here + 1 - c, z)
    firsts = {o: on_first(x, y, c, z, o) for o in (1, 2, 3)}
    seconds = {o: on_second(x, y, c, z, o) for o in (1, 2, 3)}
    depth = {(k, o): (here + k, (z + o) % SIDE) for k in (0, 1) for o in (1, 2, 3)}
    up, down = firsts[1], firsts[3]
    all_here = greet([sibling, up, down, seconds[1], seconds[3]] + list(depth.values()))

    loads = [
        pltpu.make_async_copy(queries, query_v, local_sems.at[2]),
        pltpu.make_async_copy(out_grad, grad_v, local_sems.at[3]),
    ]
    for load in loads:
        load.start()
    for t in range(3):
        pair[0, t] = keys[t * BLK : (t + 1) * BLK]
        pair[1, t] = values[t * BLK : (t + 1) * BLK]
    for t in range(3):
        near[a * ROW + c * 3 + t] = pair[c, t]
    all_here()

    mine = near.at[pl.ds(a * ROW + c * 3, 3)]
    theirs = near.at[pl.ds(a * ROW + (1 - c) * 3, 3)]
    swap = remote(pair.at[1 - c], near.at[pl.ds(b * ROW + c * 3, 3)], sends, recvs, 0, sibling)
    swap.start()
    copies = [
        remote(mine, mine, sends, recvs, 1, up),
        remote(mine, mine, sends, recvs, 2, down),
    ]
    copies[0].start()
    copies[1].start()
    swap.wait_recv()
    copies += [
        remote(theirs, theirs, sends, recvs, 3, up),
        remote(theirs, theirs, sends, recvs, 4, down),
    ]
    copies[3].start()
    copies[2].start()

    def spots(r, h):
        rows = pl.ds(pl.multiple_of(r * BLK, BLK), BLK)
        return rows, pl.ds(pl.multiple_of(h * HEAD, HEAD), HEAD)

    def totals(k, _):
        rows, columns = spots(k // 4, k % 4)
        own_totals(query_v[rows, columns], grad_v[rows, columns], keys[rows], values[rows], stats, k)
        return 0

    for load in loads:
        load.wait()
    lax.fori_loop(0, 4, totals, 0)
    copies[0].wait_recv()
    below = near.at[pl.ds(((a + 3) % 4) * ROW + c * 3, 3)]
    copies.append(remote(below, below, sends, recvs, 5, up))
    copies[4].start()
    copies[3].wait_recv()
    above = near.at[pl.ds(((a + 1) % 4) * ROW + (1 - c) * 3, 3)]
    copies.append(remote(above, above, sends, recvs, 6, down))
    copies[5].start()

    def chip_at(o):
        other = (b + o) % SIDE
        return (x * 4 + other) * (1 - c) + (other * 4 + y) * c

    def pick_of(of_chip, r, s):
        return picked[(of_chip * ROW + (s // 2) * 3 + r) * 2 + s % 2]

    for r in range(3):
        for o in range(4):
            line_chip = chip_at(o)
            blocks = [pick_of(line_chip, r, s) for s in range(4)]
            for s in range(4):
                known = second_of(blocks[s], c) == b
                if s >= 2:
                    again = jnp.logical_or(blocks[s] == blocks[0], blocks[s] == blocks[1])
                    known = jnp.logical_and(known, jnp.logical_not(again))
                at_home[(r * 4 + o) * 4 + s] = jnp.where(known, near_at(blocks[s], c), -1)
    lax.fori_loop(4, 12, totals, 0)
    for k in (1, 2, 4, 5):
        copies[k].wait_recv()

    above2, below2 = seconds[1], seconds[3]

    def flow(r, m):
        place_at = pl.ds(2 * m, 2)
        target = below2 if m in (1, 4, 5) else above2
        return remote(packed[r].at[place_at], far[r].at[place_at], sends, recvs, 7 + 6 * r + m, target)

    def served(r, o, k):
        block = pick_of(chip_at(o), r, k)
        hit = second_of(block, c) == b
        return hit, near[jnp.where(hit, near_at(block, c), 0)]

    def send_round(r):
        for m, o, first in ((0, 2, 2), (1, 2, 0), (2, 1, 0), (5, 3, 2)):
            for k in range(2):
                packed[r][2 * m + k] = served(r, o, first + k)[1]
            flow(r, m).start()

    def relay_round(r):
        for m, o, first in ((3, 1, 2), (4, 3, 0)):
            flow(r, m - 3).wait_recv()
            for k in range(2):
                hit, block = served(r, o, first + k)
                packed[r][2 * m + k] = jnp.where(hit, block, far[r][2 * (m - 3) + k])
            flow(r, m).start()

    def chosen_copy(r):
        return remote(
            give.at[pl.ds(2 * r, 2)], chosen.at[pl.ds(4 * r + 2 * c, 2)], sends, recvs, 25 + r, sibling
        )

    def take_round(r):
        for m in (2, 3, 4, 5):
            flow(r, m).wait_recv()
        if r == 0:
            send_round(1)

        def pick(core, j):
            k = core * 2 + j
            block = pick_of(chip, r, k)
            o = (second_of(block, c) - b + 4) % 4
            over = jnp.logical_or(o == 1, jnp.logical_and(o == 2, k < 2))
            from_far = far[r][jnp.where(over, 8 + k, 4 + k)]
            return jnp.where(o > 0, from_far, near[near_at(block, c)])

        for j in range(2):
            give[2 * r + j] = pick(1 - c, j)
        chosen_copy(r).start()
        for j in range(2):
            chosen[4 * r + 2 * c + j] = pick(c, j)

    def part_copy(r):
        return remote(
            other_part.at[pl.ds(2 * r, 2)], parts[r].at[pl.ds(2 * c, 2)], sends, recvs, 28 + r, sibling
        )

    def give_round(r):
        for j in range(2):
            for role in range(2):
                value = acc[j, role] * SCALE if role == 0 else acc[j, role]
                low = value.astype(LOW)

                @pl.when(c == role)
                def _():
                    parts[r][2 * c + j] = low

                @pl.when(c != role)
                def _():
                    other_part[2 * r + j] = low

        part_copy(r).start()

    def back_flow(r, m):
        source, start, at, target = (
            (merged[r], 0, 8, above2),
            (merged[r], 2, 10, above2),
            (merged[r], 2, 2, below2),
            (merged[r], 0, 0, below2),
            (came[r], 8, 4, above2),
            (came[r], 2, 6, below2),
        )[m]
        return remote(
            source.at[pl.ds(start, 2)], came[r].at[pl.ds(at, 2)], sends, recvs, 31 + 6 * r + m, target
        )

    def back_round(r):
        part_copy(r).wait_recv()
        blocks = [pick_of(chip, r, s) for s in range(4)]
        for s in range(2):
            same = [blocks[k] == blocks[s] for k in (2, 3)]
            if s == 1:
                same = [jnp.logical_and(k, blocks[0] != blocks[1]) for k in same]
            extra = parts[r][jnp.where(same[0], 2, jnp.where(same[1], 3, 4))]
            merged[r][s] = (parts[r][s].astype(F32) + extra.astype(F32)).astype(LOW)
        for s in (2, 3):
            merged[r][s] = parts[r][s]
        for m in (0, 2, 1, 3):
            back_flow(r, m).start()

    def back_relay(r):
        for m in (0, 2):
            back_flow(r, m).wait_recv()
            back_flow(r, 4 + m // 2).start()

    send_round(0)
    blank = jnp.zeros((BLK, HEAD), LOW)
    for r in range(3):
        parts[r][4] = blank
        merged[r][4] = blank
        came[r][12] = blank
    relay_round(0)
    take_round(0)
    chosen_copy(0).wait_recv()

    for r in range(3):
        acc[...] = jnp.zeros_like(acc)
        rows = pl.ds(r * BLK, BLK)
        block = index * 3 + r
        live = (picked[2 * block] != block, picked[2 * block + 1] != block)

        def body(h, _):
            @pl.when(h == 1)
            def _():
                if r == 0:
                    relay_round(1)
                    send_round(2)
                if r > 0:
                    back_round(r - 1)

            @pl.when(h == 3)
            def _():
                if r < 2:
                    take_round(r + 1)
                if r > 0:
                    back_relay(r - 1)

            columns = pl.ds(pl.multiple_of(h * HEAD, HEAD), HEAD)
            part, key_grads, value_grads = pick_step(
                query_v[rows, columns],
                grad_v[rows, columns],
                [chosen[4 * r], chosen[4 * r + 1]],
                [chosen[4 * r + 2], chosen[4 * r + 3]],
                live,
                stats,
                4 * r + h,
            )
            query_part[rows, columns] = part
            for j in range(2):
                acc[j, 0] += key_grads[j]
                acc[j, 1] += value_grads[j]
            return 0

        if r == 1:
            relay_round(2)
        lax.fori_loop(0, 4, body, 0)
        give_round(r)
        if r < 2:
            chosen_copy(r + 1).wait_recv()

    height = query_out.shape[0]
    width = query_grad.shape[1]

    def query_copy(h, o):
        source = query_grad.at[pl.ds(((z + o) % SIDE) * height, height), spots(0, h)[1]]
        target = query_out.at[:, pl.ds(pl.multiple_of(z * width + h * HEAD, HEAD), HEAD)]
        if o == 0:
            return pltpu.make_async_copy(source, target, local_sems.at[4 + h])
        return remote(
            source, target, query_sems, query_recvs, 3 * h + o - 1, (index, (z + o) % SIDE)
        )

    own[...] = jnp.zeros_like(own)
    back_round(2)

    def round_sum(r, t, rows=pl.ds(0, BLK)):
        total = None
        for o in range(4):
            start = (r * 4 + o) * 4
            base = max(o - 1, 0) * 4
            spot = 4 if o == 0 else 12
            for s in (3, 2, 1, 0):
                spot = jnp.where(at_home[start + s] == t, base + s, spot)
            value = (merged[r] if o == 0 else came[r])[spot, rows].astype(F32)
            total = value if total is None else total + value
        return total

    def early(t, _):
        sums[t] = round_sum(0, t) + round_sum(1, t)
        return 0

    half = BLK // 2
    halves = (pl.ds(0, half), pl.ds(half, half))
    plans = ((2, 0), (2, 1), (1, 1), (3, 0), (1, 0), (3, 1))

    def homeward(k, m):
        target = down if m in (1, 3, 5) else up
        return remote(
            to_first.at[6 * k + m], from_first.at[6 * k + m], sends, recvs, 50 + 6 * k + m, target
        )

    def send_home(k, m):
        o, side = plans[m]
        start = ((a + o) % SIDE) * ROW + k * 3
        if m >= 4:
            homeward(k, m - 4).wait_recv()

        def one(t, _):
            total = sums[start + t, halves[side]] + round_sum(2, start + t, halves[side])
            if m >= 4:
                total += from_first[6 * k + m - 4, t].astype(F32)
            to_first[6 * k + m, t] = total.astype(LOW)
            return 0

        lax.fori_loop(0, 3, one, 0)
        homeward(k, m).start()

    def tail(h, _):
        @pl.when(h == 1)
        def _():
            back_relay(2)
            for r in (0, 1):
                for m in (1, 3, 4, 5):
                    back_flow(r, m).wait_recv()
            lax.fori_loop(0, LINE, early, 0)
            for m in (1, 3, 4, 5):
                back_flow(2, m).wait_recv()
            for k, m in ((0, 0), (0, 1), (0, 2), (0, 3), (1, 0), (1, 1)):
                send_home(k, m)

        @pl.when(h == 2)
        def _():
            for k, m in ((0, 4), (0, 5), (1, 2), (1, 3)):
                send_home(k, m)

        @pl.when(h == 3)
        def _():
            for m in (4, 5):
                send_home(1, m)

        def one(r, _):
            rows, columns = spots(r, h)
            low, key_grad, value_grad = own_step(
                query_v[rows, columns],
                grad_v[rows, columns],
                keys[rows],
                values[rows],
                query_part[rows, columns],
                stats,
                4 * r + h,
            )
            query_grad[rows, columns] = low
            own[0, r] += key_grad * SCALE
            own[1, r] += value_grad
            return 0

        lax.fori_loop(0, 3, one, 0)
        for o in (2, 1, 3, 0):
            query_copy(h, o).start()
        return 0

    lax.fori_loop(0, 4, tail, 0)
    swap_own = remote(own.at[1 - c], own_far, sends, recvs, 49, sibling)
    swap_own.start()

    def stays(t, _):
        home[t] = sums[a * ROW + t] + round_sum(2, a * ROW + t)
        return 0

    lax.fori_loop(0, ROW, stays, 0)
    swap_own.wait_recv()

    def add_own(t, _):
        home[c * 3 + t] += own[c, t]
        home[(1 - c) * 3 + t] += own_far[t]
        return 0

    lax.fori_loop(0, 3, add_own, 0)

    finals = []
    columns = pl.ds(pl.multiple_of(z * HEAD, HEAD), HEAD)
    for k in (0, 1):
        for m in (2, 3, 4, 5):
            homeward(k, m).wait_recv()

        def finish(t, _):
            for side, pair_of in ((0, (3, 4)), (1, (2, 5))):
                total = home[k * 3 + t, halves[side]]
                for m in pair_of:
                    total += from_first[6 * k + m, t].astype(F32)
                rows = pl.ds(pl.multiple_of(t * BLK + side * half, half), half)
                done[k, rows] = total.astype(LOW)
            return 0

        lax.fori_loop(0, 3, finish, 0)
        for o in (2, 1, 3):
            copy = remote(
                done.at[k, pl.ds(((z + o) % SIDE) * height, height)],
                landed.at[c, :, columns],
                final_sends.at[k],
                final_recvs.at[c],
                o,
                depth[k, o],
            )
            copy.start()
            finals.append(copy)
    cross = remote(
        done.at[1 - c, pl.ds(z * height, height)],
        landed.at[c, :, columns],
        final_sends.at[1 - c],
        final_recvs.at[c],
        0,
        sibling,
    )
    cross.start()
    keep = pltpu.make_async_copy(
        done.at[c, pl.ds(z * height, height)], landed.at[c, :, columns], local_sems.at[1]
    )
    keep.start()
    keep.wait()
    for role in (0, 1):
        for o in (1, 2, 3):
            remote(
                done.at[0, pl.ds(0, height)],
                landed.at[role, :, pl.ds(0, HEAD)],
                final_sends.at[0],
                final_recvs.at[role],
                o,
                sibling,
            ).wait_recv()
    remote(
        done.at[0, pl.ds(0, height)],
        landed.at[1 - c, :, columns],
        final_sends.at[0],
        final_recvs.at[1 - c],
        0,
        sibling,
    ).wait_recv()
    key_out[...] = landed[0]
    value_out[...] = landed[1]
    for h in range(4):
        for o in range(4):
            query_copy(h, o).wait()
    ends = [swap, swap_own] + copies + finals + [cross] + [homeward(k, m) for k in (0, 1) for m in range(6)]
    for r in range(3):
        ends += [chosen_copy(r), part_copy(r)]
        ends += [flow(r, m) for m in range(6)] + [back_flow(r, m) for m in range(6)]
    for copy in ends:
        copy.wait_send()


def per_device(queries, key_rows, value_rows, out_grad, picked):
    vmem = pl.BlockSpec(memory_space=pltpu.VMEM)
    anywhere = pl.BlockSpec(memory_space=pl.ANY)
    tile = (BLK, HEAD)
    tokens, width = queries.shape
    height = tokens // SIDE
    dma = pltpu.SemaphoreType.DMA

    def blocks(count, kind=LOW):
        return pltpu.VMEM((count,) + tile, kind)

    return tuple(
        pl.pallas_call(
            kernel,
            out_shape=[
                jax.ShapeDtypeStruct((height, SIDE * width), LOW),
                jax.ShapeDtypeStruct((height, SIDE * HEAD), LOW),
                jax.ShapeDtypeStruct((height, SIDE * HEAD), LOW),
            ],
            in_specs=[pl.BlockSpec(memory_space=pltpu.SMEM), anywhere, vmem, vmem, anywhere],
            out_specs=[anywhere, vmem, vmem],
            scratch_shapes=[
                pltpu.VMEM((tokens, width), LOW),
                pltpu.VMEM((tokens, width), LOW),
                pltpu.VMEM((tokens, width), LOW),
                pltpu.VMEM((tokens, width), F32),
                pltpu.VMEM((12, 8, BLK), F32),
                pltpu.VMEM((2, 3) + tile, LOW),
                blocks(LINE),
                blocks(6),
                blocks(12),
                pltpu.VMEM((2, 2) + tile, F32),
                pltpu.VMEM((2, 3) + tile, F32),
                blocks(3, F32),
                blocks(6),
                blocks(LINE, F32),
                pltpu.VMEM((12, 3, BLK // 2, HEAD), LOW),
                pltpu.VMEM((12, 3, BLK // 2, HEAD), LOW),
                blocks(ROW, F32),
                pltpu.VMEM((2, 3 * BLK, HEAD), LOW),
                pltpu.VMEM((2, height, SIDE * HEAD), LOW),
                pltpu.SMEM((48,), jnp.int32),
                dma((62,)),
                dma((62,)),
                dma((12,)),
                dma((12,)),
                dma((2, 4)),
                dma((2, 4)),
                dma((8,)),
            ]
            + [blocks(12)] * 6
            + [blocks(5)] * 6
            + [blocks(13)] * 3,
            compiler_params=pltpu.CompilerParams(
                collective_id=0, has_side_effects=True, vmem_limit_bytes=VMEM_LIMIT
            ),
            name="attend",
        )(picked.reshape(-1), queries, key_rows, value_rows, out_grad)
    )


def solution(mesh):
    return jax.shard_map(
        per_device,
        mesh=mesh,
        in_specs=(P("ctx", "kvh"), P("ctx", "kvh"), P("ctx", "kvh"), P("ctx", "kvh"), P()),
        out_specs=(P(("ctx", "kvh"), None), P(("ctx", "kvh"), None), P(("ctx", "kvh"), None)),
        check_vma=False,
    )
```
